256 devices in a mesh: wide: 32 (over z_hi, x, y), narrow: 8 (over z_lo, core).
Axes of the slice: x: 4, y: 4, z: 8 (z_hi: 2, z_lo: 4; z = z_hi * 4 + z_lo), core: 2. Of those that a mesh axis runs over, the one named last changes fastest.
Arguments:
- latent: float32 [2, 256, 512, 512], P(None, 'wide', 'narrow'), may hold values from -6 to 6
- context: bfloat16 [2, 128, 256, 256], P(None, 'wide', 'narrow'), may hold values from -6 to 6
- conv_weight: bfloat16 [3, 3, 256, 512], replicated, may hold values from -0.125 to 0.125
- window_qkv: bfloat16 [512, 1536], replicated, may hold values from -0.25 to 0.25
- window_out: bfloat16 [512, 512], replicated, may hold values from -0.25 to 0.25
- window_bias: float32 [16, 15, 15], replicated, may hold values from -9 to 320
- grid_qkv: bfloat16 [512, 1536], replicated, may hold values from -0.25 to 0.25
- grid_out: bfloat16 [512, 512], replicated, may hold values from -0.25 to 0.25
- grid_bias: float32 [16, 15, 15], replicated, may hold values from -9 to 320
- mlp_gain: float32 [512], replicated, may hold values from 0.1 to 1.9
- mlp_in: bfloat16 [512, 2048], replicated, may hold values from -0.25 to 0.25
- mlp_out: bfloat16 [2048, 512], replicated, may hold values from -0.125 to 0.125
Outputs:
- forecast: float32 [2, 256, 512, 512], P(None, 'wide', 'narrow')
The draws below stay inside these ranges and needn't reach their ends.
All inputs are finite; a program needn't handle non-finite values.
Results may differ from the reference program's by a relative error of at most 0.0055.
Values may be sent and summed in bfloat16 or wider, within the bound.
A program may use at most 128 MiB of HBM per device.

```python
import jax
import jax.numpy as jnp
from jax import lax

C = 512
HEAD = 32
HEADS = 16
FFN = 2048
CC = 256
WIN = 8
BATCH = 2
H = 256
W = 512


def bias_entries(key):
    span_count = 2 * WIN - 1
    entries = 1.5 * jax.random.normal(key, (HEADS, span_count, span_count), jnp.float32)
    entries = jnp.clip(entries, -9.0, 9.0)
    return entries


def draw_window_bias(key, part):
    return bias_entries(jax.random.fold_in(key, 17))


def draw_grid_bias(key, part):
    return bias_entries(jax.random.fold_in(key, 29))


def block_scale(stream_key, shape, cuts, least, largest):
    factor_of, own = 1.0, jax.random.fold_in(stream_key, 6)
    for dim, parts in cuts:
        draws = jnp.exp(jax.random.uniform(jax.random.fold_in(own, dim), (parts,), jnp.float32, least / len(cuts), largest / len(cuts)))
        factor_of = factor_of * jnp.repeat(draws, shape[dim] // parts).reshape([-1 if axis == dim else 1 for axis in range(len(shape))])
    return factor_of


def centred(key, shape, deviation, limit, shards=(), kind=jnp.bfloat16):
    values = jax.random.normal(key, shape, jnp.float32) * deviation
    if len(shards) > 0:
        values = block_scale(key, shape, shards, -0.22, 0.18) * values
    return jnp.clip(values, min=-limit, max=limit).astype(kind)


def setup_inputs(seed: int = 0) -> dict:
    splits = jax.random.split(jax.random.key(seed), 13)
    return {
        "latent": centred(splits[0], (BATCH, H, W, C), 1.0, 6.0, ((1, 32), (2, 8)), jnp.float32),
        "context": centred(splits[1], (BATCH, H // 2, W // 2, CC), 1.0, 6.0, ((1, 32), (2, 8))),
        "conv_weight": centred(splits[2], (3, 3, CC, C), (9 * CC) ** -0.5, 0.125),
        "window_qkv": centred(splits[3], (C, 3 * C), C ** -0.5, 0.25),
        "window_out": centred(splits[4], (C, C), C ** -0.5, 0.25),
        "window_bias": draw_window_bias(jax.random.fold_in(splits[12], 71), 0),
        "grid_qkv": centred(splits[6], (C, 3 * C), C ** -0.5, 0.25),
        "grid_out": centred(splits[7], (C, C), C ** -0.5, 0.25),
        "grid_bias": draw_grid_bias(jax.random.fold_in(splits[12], 71), 0),
        "mlp_gain": jnp.clip(1.0 + 0.18 * jax.random.normal(splits[9], (C,), jnp.float32), 0.1, 1.9),
        "mlp_in": centred(splits[10], (C, FFN), C ** -0.5, 0.25),
        "mlp_out": centred(splits[11], (FFN, C), FFN ** -0.5, 0.125),
    }


NORM_EPS = 1e-05

def layer_norm(values):
    center = values - lax.optimization_barrier(jnp.mean(values, axis=-1, keepdims=True))
    spread = lax.optimization_barrier(jnp.mean(center * center, axis=-1, keepdims=True))
    return center * lax.rsqrt(spread + NORM_EPS)

def bias_lookup(bias_table):
    span_count = bias_table.shape[1]
    side_count = (span_count + 1) // 2
    places = jnp.arange(side_count * side_count, dtype=jnp.int32)
    row_of = places // side_count
    col_of = places % side_count
    row_step = row_of[:, None] - row_of[None, :] + side_count - 1
    col_step = col_of[:, None] - col_of[None, :] + side_count - 1
    return bias_table[:, row_step, col_step]

def project(values, weight):
    flat = values.reshape(-1, values.shape[-1])
    result = jnp.dot(flat, weight, preferred_element_type=jnp.float32)
    return result.reshape(values.shape[:-1] + (weight.shape[1],))

def upsample(padded, along):
    cell_count = padded.shape[along] - 2
    lower_rows = lax.slice_in_dim(padded, 0, cell_count, axis=along)
    middle = lax.slice_in_dim(padded, 1, cell_count + 1, axis=along)
    even_terms = 0.25 * lower_rows + 0.75 * middle
    upper_rows = lax.slice_in_dim(padded, 2, cell_count + 2, axis=along)
    odd_terms = 0.75 * middle + 0.25 * upper_rows
    paired = jnp.stack([even_terms, odd_terms], axis=along + 1)
    merged_shape = list(even_terms.shape)
    merged_shape[along] = 2 * cell_count
    return paired.reshape(merged_shape)

def to_windows(tiles, side_count):
    samples, row_count, col_count, channels = tiles.shape
    unfolded = tiles.reshape(samples, row_count // side_count, side_count, col_count // side_count, side_count, channels)
    return unfolded.transpose(0, 1, 3, 2, 4, 5).reshape(-1, side_count * side_count, channels)

def from_windows(grouped, samples, row_count, col_count, side_count):
    channels = grouped.shape[-1]
    unfolded = grouped.reshape(samples, row_count // side_count, col_count // side_count, side_count, side_count, channels)
    return unfolded.transpose(0, 1, 3, 2, 4, 5).reshape(samples, row_count, col_count, channels)

def to_grid(tiles, side_count):
    samples, row_count, col_count, channels = tiles.shape
    unfolded = tiles.reshape(samples, side_count, row_count // side_count, side_count, col_count // side_count, channels)
    return unfolded.transpose(0, 2, 4, 1, 3, 5).reshape(-1, side_count * side_count, channels)

def from_grid(grouped, samples, row_count, col_count, side_count):
    channels = grouped.shape[-1]
    unfolded = grouped.reshape(samples, row_count // side_count, col_count // side_count, side_count, side_count, channels)
    return unfolded.transpose(0, 3, 1, 4, 2, 5).reshape(samples, row_count, col_count, channels)

def attend(queries, key_rows, value_rows, bias_full, head_size):
    groups, members, channels = queries.shape
    head_count = channels // head_size
    query_heads = queries.astype(jnp.float32).reshape(groups, members, head_count, head_size)
    key_heads = key_rows.astype(jnp.float32).reshape(groups, members, head_count, head_size)
    value_heads = value_rows.astype(jnp.float32).reshape(groups, members, head_count, head_size)
    scores = jnp.einsum('gqhd,gkhd->ghqk', query_heads, key_heads, precision=lax.Precision.HIGHEST)
    scores = scores * head_size ** (-0.5) + bias_full[None]
    highest = lax.optimization_barrier(jnp.max(scores, axis=-1, keepdims=True))
    lifted = jnp.exp(scores - highest)
    weights = lax.optimization_barrier((lifted / lax.optimization_barrier(jnp.sum(lifted, axis=-1, keepdims=True))).astype(jnp.bfloat16))
    blended = jnp.einsum('ghqk,gkhd->gqhd', weights.astype(jnp.float32), value_heads, precision=lax.Precision.HIGHEST)
    return blended.astype(jnp.bfloat16).reshape(groups, members, channels)

def grouped_attention(grouped, weight, bias_full, head_size):
    groups, members, channels = grouped.shape
    projected = jnp.dot(grouped.reshape(groups * members, channels), weight, preferred_element_type=jnp.float32)
    projected = lax.optimization_barrier(projected.astype(jnp.bfloat16)).reshape(groups, members, 3 * channels)
    return attend(projected[..., :channels], projected[..., channels:2 * channels], projected[..., 2 * channels:], bias_full, head_size)

def blocked_attention(grouped, weight, bias_full, head_size):
    group_count, members, channels = grouped.shape
    blocks = grouped.reshape(group_count // 64, 64, members, channels)
    result = lax.map(lambda block_rows: grouped_attention(block_rows, weight, bias_full, head_size), blocks)
    return result.reshape(group_count, members, channels)

def reference(latent, context, conv_weight, window_qkv, window_out, window_bias, grid_qkv, grid_out, grid_bias, mlp_gain, mlp_in, mlp_out):
    window_table = bias_lookup(window_bias)
    grid_table = bias_lookup(grid_bias)

    def one_sample(inputs):
        fine_grid, coarse = inputs
        row_count, col_count, channels = fine_grid.shape
        computed = lax.conv_general_dilated(coarse[None].astype(jnp.float32), conv_weight.astype(jnp.float32), (1, 1), ((1, 1), (1, 1)), dimension_numbers=('NHWC', 'HWIO', 'NHWC'), precision=lax.Precision.HIGHEST)
        features = lax.optimization_barrier(computed.astype(jnp.bfloat16))
        padded = jnp.pad(features, ((0, 0), (1, 1), (1, 1), (0, 0))).astype(jnp.float32)
        lifted_rows = upsample(padded, 1)
        lifted_rows = jnp.pad(lifted_rows, ((0, 0), (0, 0), (0, 0), (0, 0)))
        upsampled = upsample(lifted_rows, 2)
        residual_a = fine_grid[None] + upsampled
        normed = layer_norm(residual_a).astype(jnp.bfloat16)
        window_heads = from_windows(blocked_attention(to_windows(normed, WIN), window_qkv, window_table, HEAD), 1, row_count, col_count, WIN)
        residual_b = residual_a + project(window_heads, window_out)
        normed = layer_norm(residual_b).astype(jnp.bfloat16)
        grid_heads = from_grid(blocked_attention(to_grid(normed, WIN), grid_qkv, grid_table, HEAD), 1, row_count, col_count, WIN)
        residual_c = residual_b + project(grid_heads, grid_out)
        normed = (layer_norm(residual_c) * mlp_gain).astype(jnp.bfloat16)
        hidden = jax.nn.gelu(project(normed, mlp_in)).astype(jnp.bfloat16)
        return (residual_c + project(hidden, mlp_out))[0]
    return lax.map(one_sample, (latent, context))
```

```python
import math

import jax
import jax.numpy as jnp
from jax import lax
from jax.experimental import pallas as pl
from jax.experimental.pallas import tpu as pltpu
from jax.sharding import PartitionSpec as P

MESH = pl.DeviceIdType.MESH
F32 = jnp.float32
BF16 = jnp.bfloat16
NORM_EPS = 1e-05
HEAD = 32
WIN = 8
CELLS = WIN * WIN
LOG2E = 1.4426950408889634
CTX_COLS = 48


def iota(shape, dim):
    return lax.broadcasted_iota(jnp.int32, shape, dim)


def dot_nn(a, b):
    return jnp.dot(a, b, preferred_element_type=F32)


def dot_nt(a, b):
    return lax.dot_general(a, b, (((1,), (1,)), ((), ())), preferred_element_type=F32)


def layer_norm(values):
    center = values - jnp.mean(values, axis=-1, keepdims=True)
    spread = jnp.mean(center * center, axis=-1, keepdims=True)
    return center * lax.rsqrt(spread + NORM_EPS)


def identity(size):
    return jnp.where(iota((size, size), 0) == iota((size, size), 1), 1.0, 0.0).astype(BF16)


def fill_upsampler(up_ref):
    rows, depth = up_ref.shape
    lane = iota((1, depth), 1)
    coarse_row = jnp.zeros((1, depth), jnp.int32)
    for step in range(1, depth // CTX_COLS):
        coarse_row = coarse_row + jnp.where(lane >= step * CTX_COLS, 1, 0)
    coarse_col = lane - coarse_row * CTX_COLS
    block = 64
    for start in range(0, rows, block):
        fine_row = start // 64
        row_centre = fine_row // 2 + 1
        row_other = fine_row // 2 + (2 if fine_row % 2 else 0)
        row_weight = jnp.where(coarse_row == row_centre, 0.75, 0.0) + jnp.where(
            coarse_row == row_other, 0.25, 0.0
        )
        fine_col = iota((block, depth), 0)
        col_centre = (fine_col >> 1) + 8
        col_other = col_centre + 2 * (fine_col & 1) - 1
        col_weight = jnp.where(coarse_col == col_centre, 0.75, 0.0) + jnp.where(
            coarse_col == col_other, 0.25, 0.0
        )
        up_ref[pl.ds(start, block), :] = (row_weight * col_weight).astype(BF16)


def fill_bias(table, which, spread_ref, step_ref, bias_ref):
    pick = jnp.where(iota((16, 1024), 0) == (iota((16, 1024), 1) >> 6), 1.0, 0.0)
    spread_ref[...] = (
        jnp.dot(table, pick, preferred_element_type=F32, precision=lax.Precision.HIGHEST) * LOG2E
    )
    col_step = (iota((8, 1024), 1) & 7) - iota((8, 1024), 0) + 7

    def one_row_step(a, carry):
        rows = spread_ref[pl.ds(pl.multiple_of(a * 16, 16), 16), :]
        total = jnp.zeros((8, 1024), F32)
        for j in range(15):
            total = jnp.where(col_step == j, jnp.broadcast_to(rows[j : j + 1], (8, 1024)), total)
        step_ref[a] = total
        return carry

    lax.fori_loop(0, 15, one_row_step, 0)
    query_row = (iota((8, 1024), 1) >> 3) & 7

    def one_key_row(rq, carry):
        total = jnp.zeros((8, 1024), F32)
        for rp in range(8):
            total = jnp.where(query_row == rp, step_ref[rp - rq + 7], total)
        for block in range(4):
            bias_ref[which, block, pl.ds(pl.multiple_of(rq * 8, 8), 8), :] = total[
                :, block * 256 : (block + 1) * 256
            ]
        return carry

    lax.fori_loop(0, 8, one_key_row, 0)


def attend(x, qkv_ref, value_ref, bias_ref, which):
    width = x.shape[1]
    queries = dot_nn(x, qkv_ref[:, 0:width]).astype(BF16)
    keys = dot_nn(x, qkv_ref[:, width : 2 * width]).astype(BF16)
    values = dot_nt(value_ref[which], x).astype(BF16)
    head_of_lane = iota((CELLS, 128), 1) >> 5
    head_masks = [jnp.where(head_of_lane == h, 1.0, 0.0).astype(BF16) for h in range(4)]
    group_of_lane = iota((128, 256), 1) >> 6
    group_masks = [jnp.where(group_of_lane == g, 1.0, 0.0).astype(BF16) for g in range(4)]
    low = iota((HEAD, 128), 1) < 64
    outs = []
    for block in range(width // 128):
        lanes = slice(block * 128, (block + 1) * 128)
        bias = bias_ref[which, block]
        weights = []
        for g in range(4):
            rows = slice(g * CELLS, (g + 1) * CELLS)
            query = queries[rows, lanes]
            spread = jnp.concatenate([query * mask for mask in head_masks], axis=0)
            scores = dot_nt(keys[rows, lanes], spread) * (LOG2E * HEAD**-0.5) + bias
            lifted = jnp.exp2(scores - jnp.max(scores, axis=0, keepdims=True))
            inverse = 1.0 / jnp.sum(lifted, axis=0, keepdims=True)
            weights.append((lifted * inverse).astype(BF16))
        weight = jnp.concatenate(weights, axis=0)
        value = values[lanes]
        stacked = jnp.concatenate([value * mask for mask in group_masks], axis=0)
        blended = dot_nn(stacked, weight)
        for h in range(4):
            picked = []
            for pair in range(2):
                parts = []
                for g in (2 * pair, 2 * pair + 1):
                    parts.append(
                        blended[
                            g * 128 + h * HEAD : g * 128 + (h + 1) * HEAD,
                            (h // 2) * 128 : (h // 2 + 1) * 128,
                        ]
                    )
                first, second = parts
                if h % 2 == 0:
                    picked.append(jnp.where(low, first, pltpu.roll(second, 64, 1)))
                else:
                    picked.append(jnp.where(low, pltpu.roll(first, 64, 1), second))
            outs.append(jnp.concatenate(picked, axis=1).astype(BF16))
    turned = jnp.concatenate(outs, axis=0)
    return dot_nt(identity(4 * CELLS), turned).astype(BF16)


def block_kernel(
    latent_ref,
    context_ref,
    conv_hbm,
    window_qkv_hbm,
    window_out_hbm,
    grid_qkv_hbm,
    grid_out_hbm,
    mlp_in_hbm,
    mlp_out_hbm,
    table_ref,
    gain_ref,
    out_ref,
    res,
    halo,
    conv_w,
    window_qkv,
    window_out,
    grid_qkv,
    grid_out,
    mlp_in,
    mlp_out,
    value_t,
    up,
    bias,
    spread,
    steps,
    perm,
    sent,
    received,
    answers,
    returned,
    grouped,
    heads_buf,
    load_sem,
    halo_send,
    halo_recv,
    there_send,
    there_recv,
    back_send,
    back_recv,
    out_sem,
):
    wide = lax.axis_index("wide")
    narrow = lax.axis_index("narrow")
    wide_count = lax.axis_size("wide")
    narrow_count = lax.axis_size("narrow")
    planes = wide_count // WIN
    plane = lax.rem(wide, planes)
    my_row = wide // planes
    me = my_row * WIN + narrow

    def device(place):
        return ((place // WIN) * planes + plane, lax.rem(place, WIN))

    loads = [
        pltpu.make_async_copy(source, target, load_sem.at[i])
        for i, (source, target) in enumerate(
            (
                (conv_hbm, conv_w),
                (latent_ref, res),
                (window_qkv_hbm, window_qkv),
                (window_out_hbm, window_out),
                (grid_qkv_hbm, grid_qkv),
                (grid_out_hbm, grid_out),
                (mlp_in_hbm, mlp_in),
                (mlp_out_hbm, mlp_out),
            )
        )
    ]
    own = pltpu.make_async_copy(context_ref, halo.at[:, pl.ds(2, 4), pl.ds(16, 32), :], halo_recv)
    own.start()

    barrier = pltpu.get_barrier_semaphore()

    def greet(i, carry):
        pl.semaphore_signal(
            barrier, inc=1, device_id=device(lax.rem(me + i, CELLS)), device_id_type=MESH
        )
        return carry

    around = []
    for dw in (-1, 0, 1):
        for dn in (-1, 0, 1):
            if dw or dn:
                around.append((dw, dn))

    def neighbour(dw, dn):
        return (
            lax.rem(wide + dw + wide_count, wide_count),
            lax.rem(narrow + dn + narrow_count, narrow_count),
        )

    for dw, dn in around:
        if dw:
            pl.semaphore_signal(barrier, inc=1, device_id=neighbour(dw, dn), device_id_type=MESH)
    lax.fori_loop(1, CELLS, greet, 0)
    for load in loads:
        load.start()
    pl.semaphore_wait(barrier, CELLS - 1 + 6)

    sends = []
    row_cut = {-1: (0, 2, 6), 0: (0, 4, 2), 1: (2, 2, 0)}
    col_cut = {-1: (0, 16, 48), 0: (0, 32, 16), 1: (16, 16, 0)}
    for dw, dn in around:
        row_from, rows, row_to = row_cut[dw]
        col_from, cols, col_to = col_cut[dn]
        copy = pltpu.make_async_remote_copy(
            src_ref=context_ref.at[:, pl.ds(row_from, rows), pl.ds(col_from, cols), :],
            dst_ref=halo.at[:, pl.ds(row_to, rows), pl.ds(col_to, cols), :],
            send_sem=halo_send.at[len(sends)],
            recv_sem=halo_recv,
            device_id=neighbour(dw, dn),
            device_id_type=MESH,
        )
        copy.start()
        sends.append(copy)

    fill_upsampler(up)
    out_row = iota((256, 256), 0)
    in_row = iota((256, 256), 1)
    perm[0] = jnp.where(
        in_row == (out_row & 15) * 16 + (out_row >> 7) * 8 + ((out_row >> 4) & 7), 1.0, 0.0
    ).astype(BF16)
    perm[1] = jnp.where(
        out_row == (in_row & 15) * 16 + (in_row >> 7) * 8 + ((in_row >> 4) & 7), 1.0, 0.0
    ).astype(BF16)
    fill_bias(table_ref[0], 0, spread, steps, bias)
    fill_bias(table_ref[1], 1, spread, steps, bias)
    width = window_out.shape[0]
    loads[2].wait()
    value_t[0] = dot_nt(identity(width), window_qkv[:, 2 * width :]).astype(BF16)
    loads[4].wait()
    value_t[1] = dot_nt(identity(width), grid_qkv[:, 2 * width :]).astype(BF16)

    pltpu.make_async_copy(halo, halo, halo_recv).wait()
    loads[0].wait()
    loads[1].wait()
    depth = context_ref.shape[3]
    half_rows, half_cols = context_ref.shape[1], context_ref.shape[2]
    batch = latent_ref.shape[0]

    def convolve(b, carry):
        widened = halo[b].astype(F32)[:, 8:56, :]
        shape = (8, CTX_COLS, depth)
        row_place = wide * half_rows - 2 + iota(shape, 0)
        col_place = narrow * half_cols - 8 + iota(shape, 1)
        inside = (
            (row_place >= 0)
            & (row_place < wide_count * half_rows)
            & (col_place >= 0)
            & (col_place < narrow_count * half_cols)
        )
        widened = jnp.where(inside, widened, 0.0).astype(BF16)
        rows = 6 * CTX_COLS
        tall = jnp.concatenate([widened[i : i + 6].reshape(rows, depth) for i in range(3)], axis=1)
        left, centre, right = [
            dot_nn(tall, conv_w[:, dl].reshape(3 * depth, width)) for dl in range(3)
        ]
        total = centre + pltpu.roll(left, 1, 0) + pltpu.roll(right, rows - 1, 0)
        shape = (6, CTX_COLS, width)
        row_place = wide * half_rows - 1 + iota(shape, 0)
        col_place = narrow * half_cols - 8 + iota(shape, 1)
        inside = (
            (row_place >= 0)
            & (row_place < wide_count * half_rows)
            & (col_place >= 0)
            & (col_place < narrow_count * half_cols)
        )
        features = jnp.where(inside.reshape(rows, width), total, 0.0).astype(BF16)
        res[b] = res[b] + dot_nn(up[...], features).reshape(res.shape[1:])
        return carry

    lax.fori_loop(0, batch, convolve, 0)
    loads[3].wait()

    def windows(step, carry):
        b, half = step // 2, lax.rem(step, 2)
        places = [lax.rem(narrow + half * 4 + i, WIN) for i in range(4)]
        before = jnp.concatenate([res[b, :, place].reshape(CELLS, width) for place in places], axis=0)
        normed = layer_norm(before).astype(BF16)
        heads = attend(normed, window_qkv, value_t, bias, 0)
        after = before + dot_nn(heads, window_out[...])
        normed = layer_norm(after).reshape(4, WIN, WIN, width)
        for i, place in enumerate(places):
            res[b, :, place] = after[i * CELLS : (i + 1) * CELLS].reshape(WIN, WIN, width)
            sent[b, place] = jnp.concatenate(
                [normed[i, :, :, : width // 2], normed[i, :, :, width // 2 :]], axis=1
            ).astype(BF16)

        def post(i, carry):
            place = lax.rem(narrow + half * 4 + i // WIN, WIN)
            row = lax.rem(my_row + lax.rem(i, WIN), WIN)
            target = row * WIN + place

            @pl.when(target == me)
            def _():
                pltpu.make_async_copy(
                    sent.at[b, place, row], received.at[b, me], there_recv.at[b]
                ).start()

            @pl.when(target != me)
            def _():
                pltpu.make_async_remote_copy(
                    src_ref=sent.at[b, place, row],
                    dst_ref=received.at[b, me],
                    send_sem=there_send.at[b],
                    recv_sem=there_recv.at[b],
                    device_id=device(target),
                    device_id_type=MESH,
                ).start()

            return carry

        lax.fori_loop(0, 4 * WIN, post, 0)
        return carry

    lax.fori_loop(0, 2 * batch, windows, 0)

    def grid(b, carry):
        pltpu.make_async_copy(received.at[b], received.at[b], there_recv.at[b]).wait()
        half_width = width // 2
        for chunk in range(4):
            rows = received[b, chunk * 16 : (chunk + 1) * 16].reshape(256, half_width)
            turned = dot_nn(perm[0], rows).astype(BF16)
            for half in range(2):
                grouped[:, chunk * 16 : (chunk + 1) * 16, half * half_width : (half + 1) * half_width] = (
                    turned[half * 128 : (half + 1) * 128].reshape(WIN, 16, half_width)
                )

        def groups(part, carry):
            start = part * 4
            x = grouped[pl.ds(start, 4)].reshape(4 * CELLS, width)
            heads = attend(x, grid_qkv, value_t, bias, 1)
            heads_buf[pl.ds(start, 4)] = heads.reshape(4, CELLS, width)
            return carry

        lax.fori_loop(0, 2, groups, 0)
        for chunk in range(4):
            rows = jnp.concatenate(
                [
                    heads_buf[
                        :, chunk * 16 : (chunk + 1) * 16, half * half_width : (half + 1) * half_width
                    ].reshape(128, half_width)
                    for half in range(2)
                ],
                axis=0,
            )
            answers[b, chunk * 16 : (chunk + 1) * 16] = (
                dot_nn(perm[1], rows).astype(BF16).reshape(16, 16, half_width)
            )

        pltpu.make_async_copy(answers.at[b, me], returned.at[b, me], back_recv.at[b]).start()

        def post(i, carry):
            target = lax.rem(me + i, CELLS)
            pltpu.make_async_remote_copy(
                src_ref=answers.at[b, target],
                dst_ref=returned.at[b, me],
                send_sem=back_send.at[b],
                recv_sem=back_recv.at[b],
                device_id=device(target),
                device_id_type=MESH,
            ).start()
            return carry

        lax.fori_loop(1, CELLS, post, 0)
        return carry

    lax.fori_loop(0, batch, grid, 0)
    loads[5].wait()
    loads[6].wait()
    loads[7].wait()
    gain = gain_ref[...]

    def mlp(step, carry):
        b, half = step // 2, lax.rem(step, 2)

        @pl.when(half == 0)
        def _():
            pltpu.make_async_copy(returned.at[b], returned.at[b], back_recv.at[b]).wait()

        packed = returned[b, pl.ds(pl.multiple_of(half * 32, 32), 32)].astype(F32)
        heads = jnp.concatenate([packed[:, :8], packed[:, 8:]], axis=2)
        heads = heads.reshape(4 * CELLS, width).astype(BF16)
        start = half * 4
        total = res[b, pl.ds(start, 4)].reshape(4 * CELLS, width) + dot_nn(heads, grid_out[...])
        normed = (layer_norm(total) * gain).astype(BF16)
        cut = 512
        for i in range(mlp_in.shape[1] // cut):
            inner = dot_nn(normed, mlp_in[:, i * cut : (i + 1) * cut])
            cubic = inner + 0.044715 * (inner * inner * inner)
            hidden = 0.5 * inner * (1.0 + jnp.tanh(math.sqrt(2.0 / math.pi) * cubic))
            total = total + dot_nn(hidden.astype(BF16), mlp_out[i * cut : (i + 1) * cut, :])
        res[b, pl.ds(start, 4)] = total.reshape(4, WIN, WIN, width)
        pltpu.make_async_copy(
            res.at[b, pl.ds(start, 4)], out_ref.at[b, pl.ds(start, 4)], out_sem
        ).start()
        return carry

    lax.fori_loop(0, 2 * batch, mlp, 0)
    for copy in sends:
        copy.wait_send()
    for b in range(batch):
        part = received.at[b, pl.ds(0, CELLS - 1)]
        pltpu.make_async_copy(part, part, there_send.at[b]).wait()
        pltpu.make_async_copy(part, part, back_send.at[b]).wait()
    pltpu.make_async_copy(res, out_ref, out_sem).wait()


def on_device(
    latent,
    context,
    conv_weight,
    window_qkv,
    window_out,
    window_bias,
    grid_qkv,
    grid_out,
    grid_bias,
    mlp_gain,
    mlp_in,
    mlp_out,
):
    samples, row_count, col_count, channels = latent.shape
    tables = jnp.stack([window_bias, grid_bias]).transpose(0, 2, 3, 1)
    tables = jnp.pad(tables, ((0, 0), (0, 0), (0, 1), (0, 0))).reshape(2, 240, 16)
    tiles = latent.reshape(samples, row_count, col_count // WIN, WIN, channels)
    vmem = pltpu.VMEM
    dma = pltpu.SemaphoreType.DMA
    any_spec = pl.BlockSpec(memory_space=pl.ANY)
    vmem_spec = pl.BlockSpec(memory_space=pltpu.VMEM)
    slots = (samples, CELLS, 2 * WIN, channels // 2)
    result = pl.pallas_call(
        block_kernel,
        out_shape=jax.ShapeDtypeStruct(tiles.shape, F32),
        in_specs=[any_spec] * 9 + [vmem_spec] * 2,
        out_specs=any_spec,
        scratch_shapes=[
            vmem(tiles.shape, F32),
            vmem((samples, 8, 64, context.shape[3]), BF16),
            vmem(conv_weight.shape, BF16),
            vmem(window_qkv.shape, BF16),
            vmem(window_out.shape, BF16),
            vmem(grid_qkv.shape, BF16),
            vmem(grid_out.shape, BF16),
            vmem(mlp_in.shape, BF16),
            vmem(mlp_out.shape, BF16),
            vmem((2, channels, channels), BF16),
            vmem((row_count * col_count, 6 * CTX_COLS), BF16),
            vmem((2, 4, CELLS, 256), F32),
            vmem((240, 1024), F32),
            vmem((15, 8, 1024), F32),
            vmem((2, 256, 256), BF16),
            vmem((samples, WIN, WIN, 2 * WIN, channels // 2), BF16),
            vmem(slots, BF16),
            vmem(slots, BF16),
            vmem(slots, BF16),
            vmem((WIN, CELLS, channels), BF16),
            vmem((WIN, CELLS, channels), BF16),
            dma((8,)),
            dma((8,)),
            dma,
            dma((samples,)),
            dma((samples,)),
            dma((samples,)),
            dma((samples,)),
            dma,
        ],
        compiler_params=pltpu.CompilerParams(
            collective_id=0, has_side_effects=True, vmem_limit_bytes=56 * 2**20
        ),
        cost_estimate=pl.CostEstimate(
            flops=10_000_000_000, bytes_accessed=16_000_000, transcendentals=4_000_000
        ),
    )(
        tiles,
        context,
        conv_weight,
        window_qkv,
        window_out,
        grid_qkv,
        grid_out,
        mlp_in,
        mlp_out,
        tables,
        mlp_gain.reshape(1, channels),
    )
    return result.reshape(latent.shape)


def solution(mesh):
    return jax.shard_map(
        on_device,
        mesh=mesh,
        in_specs=(
            P(None, "wide", "narrow", None),
            P(None, "wide", "narrow", None),
            P(),
            P(),
            P(),
            P(),
            P(),
            P(),
            P(),
            P(),
            P(),
            P(),
        ),
        out_specs=P(None, "wide", "narrow", None),
        check_vma=False,
    )
```

```python
import math

import jax
import jax.numpy as jnp
from jax import lax
from jax.experimental import pallas as pl
from jax.experimental.pallas import tpu as pltpu
from jax.sharding import PartitionSpec as P

MESH = pl.DeviceIdType.MESH
F32 = jnp.float32
BF16 = jnp.bfloat16
NORM_EPS = 1e-05
HEAD = 32
WIN = 8
CELLS = WIN * WIN
LOG2E = 1.4426950408889634
CTX_COLS = 48
GROUP_BATCH = 4


def iota(shape, dim):
    return lax.broadcasted_iota(jnp.int32, shape, dim)


def dot_nn(a, b):
    return jnp.dot(a, b, preferred_element_type=F32)


def dot_nt(a, b):
    return lax.dot_general(a, b, (((1,), (1,)), ((), ())), preferred_element_type=F32)


def layer_norm(values):
    center = values - jnp.mean(values, axis=-1, keepdims=True)
    spread = jnp.mean(center * center, axis=-1, keepdims=True)
    return center * lax.rsqrt(spread + NORM_EPS)


def identity(size):
    return jnp.where(iota((size, size), 0) == iota((size, size), 1), 1.0, 0.0).astype(BF16)


def fill_upsampler(up_ref):
    rows, depth = up_ref.shape
    lane = iota((1, depth), 1)
    coarse_row = jnp.zeros((1, depth), jnp.int32)
    for step in range(1, depth // CTX_COLS):
        coarse_row = coarse_row + jnp.where(lane >= step * CTX_COLS, 1, 0)
    coarse_col = lane - coarse_row * CTX_COLS
    block = 64
    for start in range(0, rows, block):
        fine_row = start // 64
        row_centre = fine_row // 2 + 1
        row_other = fine_row // 2 + (2 if fine_row % 2 else 0)
        row_weight = jnp.where(coarse_row == row_centre, 0.75, 0.0) + jnp.where(
            coarse_row == row_other, 0.25, 0.0
        )
        fine_col = iota((block, depth), 0)
        col_centre = (fine_col >> 1) + 8
        col_other = col_centre + 2 * (fine_col & 1) - 1
        col_weight = jnp.where(coarse_col == col_centre, 0.75, 0.0) + jnp.where(
            coarse_col == col_other, 0.25, 0.0
        )
        up_ref[pl.ds(start, block), :] = (row_weight * col_weight).astype(BF16)


def three_terms(values):
    high = values.astype(BF16)
    rest = values - high.astype(F32)
    middle = rest.astype(BF16)
    return high, middle, (rest - middle.astype(F32)).astype(BF16)


def fill_bias(table, which, spread_ref, step_ref, bias_ref):
    turn = jnp.where(iota((16, 15), 0) == iota((16, 15), 1), 1.0, 0.0).astype(BF16)
    pick = jnp.where((iota((240, 1024), 0) & 15) == (iota((240, 1024), 1) >> 6), 1.0, 0.0)
    pick = pick.astype(BF16)
    step_of_lane = iota((16, 240), 1) >> 4
    total = jnp.zeros((240, 1024), F32)
    for term in three_terms(table.reshape(240, 15)):
        turned = dot_nt(turn, term)
        apart = [jnp.where(step_of_lane == a, turned, 0.0).astype(BF16) for a in range(15)]
        total = total + dot_nn(jnp.concatenate(apart, axis=0), pick)
    spread_ref[...] = total * LOG2E
    col_step = (iota((8, 1024), 1) & 7) - iota((8, 1024), 0) + 7

    def one_row_step(a, carry):
        rows = spread_ref[pl.ds(pl.multiple_of(a * 16, 16), 16), :]
        total = jnp.zeros((8, 1024), F32)
        for j in range(15):
            total = jnp.where(col_step == j, jnp.broadcast_to(rows[j : j + 1], (8, 1024)), total)
        step_ref[a] = total
        return carry

    lax.fori_loop(0, 15, one_row_step, 0)
    query_row = (iota((8, 1024), 1) >> 3) & 7

    def one_key_row(rq, carry):
        total = jnp.zeros((8, 1024), F32)
        for rp in range(8):
            total = jnp.where(query_row == rp, step_ref[rp - rq + 7], total)
        for block in range(4):
            bias_ref[which, block, pl.ds(pl.multiple_of(rq * 8, 8), 8), :] = total[
                :, block * 256 : (block + 1) * 256
            ]
        return carry

    lax.fori_loop(0, 8, one_key_row, 0)


def attend(x, qkv_ref, value_ref, bias_ref, which):
    width = x.shape[1]
    count = x.shape[0] // CELLS
    queries = dot_nn(x, qkv_ref[:, 0:width]).astype(BF16)
    keys = dot_nn(x, qkv_ref[:, width : 2 * width]).astype(BF16)
    values = dot_nt(value_ref[which], x).astype(BF16)
    head_of_lane = iota((CELLS, 128), 1) >> 5
    head_masks = [jnp.where(head_of_lane == h, 1.0, 0.0).astype(BF16) for h in range(4)]
    group_of_lane = iota((128, count * CELLS), 1) >> 6
    group_masks = [jnp.where(group_of_lane == g, 1.0, 0.0).astype(BF16) for g in range(count)]
    low = iota((HEAD, 128), 1) < 64
    outs = []
    for block in range(width // 128):
        lanes = slice(block * 128, (block + 1) * 128)
        bias = bias_ref[which, block]
        weights = []
        for g in range(count):
            rows = slice(g * CELLS, (g + 1) * CELLS)
            query = queries[rows, lanes]
            spread = jnp.concatenate([query * mask for mask in head_masks], axis=0)
            scores = dot_nt(keys[rows, lanes], spread) * (LOG2E * HEAD**-0.5) + bias
            lifted = jnp.exp2(scores - jnp.max(scores, axis=0, keepdims=True))
            inverse = 1.0 / jnp.sum(lifted, axis=0, keepdims=True)
            weights.append((lifted * inverse).astype(BF16))
        weight = jnp.concatenate(weights, axis=0)
        value = values[lanes]
        stacked = jnp.concatenate([value * mask for mask in group_masks], axis=0)
        blended = dot_nn(stacked, weight)
        for h in range(4):
            picked = []
            for pair in range(count // 2):
                parts = []
                for g in (2 * pair, 2 * pair + 1):
                    parts.append(
                        blended[
                            g * 128 + h * HEAD : g * 128 + (h + 1) * HEAD,
                            (h // 2) * 128 : (h // 2 + 1) * 128,
                        ]
                    )
                first, second = parts
                if h % 2 == 0:
                    picked.append(jnp.where(low, first, pltpu.roll(second, 64, 1)))
                else:
                    picked.append(jnp.where(low, pltpu.roll(first, 64, 1), second))
            outs.append(jnp.concatenate(picked, axis=1).astype(BF16))
    turned = jnp.concatenate(outs, axis=0)
    return dot_nt(identity(count * CELLS), turned).astype(BF16)


def block_kernel(
    latent_ref,
    context_ref,
    conv_hbm,
    window_qkv_hbm,
    window_out_hbm,
    grid_qkv_hbm,
    grid_out_hbm,
    mlp_in_hbm,
    mlp_out_hbm,
    window_table,
    grid_table,
    gain_ref,
    out_ref,
    res,
    halo,
    edge_out,
    edge_in,
    conv_w,
    window_qkv,
    window_out,
    grid_qkv,
    grid_out,
    mlp_in,
    mlp_out,
    value_t,
    up,
    bias,
    spread,
    steps,
    perm,
    sent,
    received,
    answers,
    returned,
    grouped,
    heads_buf,
    load_sem,
    own_sem,
    row_send,
    row_recv,
    edge_send,
    edge_recv,
    there_send,
    there_recv,
    back_send,
    back_recv,
    out_sem,
):
    wide = lax.axis_index("wide")
    narrow = lax.axis_index("narrow")
    wide_count = lax.axis_size("wide")
    narrow_count = lax.axis_size("narrow")
    planes = wide_count // WIN
    plane = lax.rem(wide, planes)
    my_row = wide // planes
    me = my_row * WIN + narrow

    def device(place):
        return ((place // WIN) * planes + plane, lax.rem(place, WIN))

    loads = [
        pltpu.make_async_copy(source, target, load_sem.at[i])
        for i, (source, target) in enumerate(
            (
                (conv_hbm, conv_w),
                (latent_ref, res),
                (window_qkv_hbm, window_qkv),
                (window_out_hbm, window_out),
                (grid_qkv_hbm, grid_qkv),
                (grid_out_hbm, grid_out),
                (mlp_in_hbm, mlp_in),
                (mlp_out_hbm, mlp_out),
            )
        )
    ]
    half_rows, half_cols = context_ref.shape[1], context_ref.shape[2]
    depth = context_ref.shape[3]
    batch = latent_ref.shape[0]
    own = pltpu.make_async_copy(context_ref, halo.at[:, pl.ds(2, half_rows)], own_sem)
    own.start()
    edge_in[...] = jnp.zeros_like(edge_in)
    for load in loads:
        load.start()

    barrier = pltpu.get_barrier_semaphore()

    def greet(i, carry):
        pl.semaphore_signal(
            barrier, inc=1, device_id=device(lax.rem(me + i, CELLS)), device_id_type=MESH
        )
        return carry

    def neighbour(dw, dn):
        return (
            lax.rem(wide + dw + wide_count, wide_count),
            lax.rem(narrow + dn + narrow_count, narrow_count),
        )

    for dw in (-1, 1):
        for dn in (0, -1, 1):
            pl.semaphore_signal(barrier, inc=1, device_id=neighbour(dw, dn), device_id_type=MESH)
    lax.fori_loop(1, CELLS, greet, 0)

    own.wait()
    for side in range(2):
        strip = halo[:, 2 : 2 + half_rows, side * 16 : side * 16 + 16, :].reshape(
            batch * half_rows * 16, depth
        )
        row = iota((16, batch * half_rows * 16), 0)
        pick = iota((16, batch * half_rows * 16), 1) == (row >> 1) * 16 + (row & 1) + 14 * side
        edge_out[side] = dot_nn(jnp.where(pick, 1.0, 0.0).astype(BF16), strip).astype(BF16)
    pl.semaphore_wait(barrier, CELLS - 1 + 6)

    def exists(dw, dn):
        return (
            (wide + dw >= 0)
            & (wide + dw < wide_count)
            & (narrow + dn >= 0)
            & (narrow + dn < narrow_count)
        )

    def row_copy(b, dw):
        lane = (dw + 1) // 2
        return pltpu.make_async_remote_copy(
            src_ref=context_ref.at[b, pl.ds(half_rows - 2 if dw > 0 else 0, 2)],
            dst_ref=halo.at[b, pl.ds(0 if dw > 0 else half_rows + 2, 2)],
            send_sem=row_send.at[b, lane],
            recv_sem=row_recv.at[b, lane],
            device_id=neighbour(dw, 0),
            device_id_type=MESH,
        )

    def edge_copy(dw, dn):
        side = (dn + 1) // 2
        return pltpu.make_async_remote_copy(
            src_ref=edge_out.at[side],
            dst_ref=edge_in.at[1 - side, 1 - dw],
            send_sem=edge_send.at[side, 1 - dw],
            recv_sem=edge_recv.at[1 - side, 1 - dw],
            device_id=neighbour(dw, dn),
            device_id_type=MESH,
        )

    edges = [(dw, dn) for dn in (-1, 1) for dw in (-1, 0, 1)]
    for dw in (-1, 1):
        pl.when(exists(dw, 0))(row_copy(0, dw).start)
    for dw, dn in edges:
        pl.when(exists(dw, dn))(edge_copy(dw, dn).start)
    for b in range(1, batch):
        for dw in (-1, 1):
            pl.when(exists(dw, 0))(row_copy(b, dw).start)

    fill_bias(window_table[...], 0, spread, steps, bias)
    fill_upsampler(up)
    width = window_out.shape[0]
    loads[2].wait()
    value_t[0] = dot_nt(identity(width), window_qkv[:, 2 * width :]).astype(BF16)
    for dw, dn in edges:
        pl.when(exists(-dw, -dn))(edge_copy(dw, dn).wait_recv)
    loads[0].wait()
    loads[1].wait()
    loads[3].wait()
    def convolve(b):
        for dw in (-1, 1):
            lane = (dw + 1) // 2
            arrived = halo.at[b, pl.ds(0 if dw > 0 else half_rows + 2, 2)]
            pl.when(exists(-dw, 0))(
                pltpu.make_async_copy(arrived, arrived, row_recv.at[b, lane]).wait
            )
        sides = []
        place, taken = iota((64, 48), 0), iota((64, 48), 1)
        row, col = place >> 3, place & 7
        slot = jnp.where(row < 2, 0, jnp.where(row < 2 + half_rows, 1, 2))
        their_row = jnp.where(row < 2, row + half_rows - 2, row - 2)
        their_row = jnp.where(row < 2 + half_rows, their_row, row - 2 - half_rows)
        base = slot * 16 + b * (2 * half_rows) + their_row * 2
        for side in range(2):
            first = 6 if side == 0 else 0
            chosen = (taken == base + col - first) & (col >= first) & (col < first + 2)
            strip = dot_nn(
                jnp.where(chosen, 1.0, 0.0).astype(BF16), edge_in[side].reshape(48, depth)
            )
            sides.append(strip.reshape(8, 8, depth))
        widened = jnp.concatenate([sides[0], halo[b].astype(F32), sides[1]], axis=1)
        shape = (8, CTX_COLS, depth)
        row_place = wide * half_rows - 2 + iota(shape, 0)
        col_place = narrow * half_cols - 8 + iota(shape, 1)
        inside = (
            (row_place >= 0)
            & (row_place < wide_count * half_rows)
            & (col_place >= 0)
            & (col_place < narrow_count * half_cols)
        )
        widened = jnp.where(inside, widened, 0.0).astype(BF16)
        rows = 6 * CTX_COLS
        tall = jnp.concatenate([widened[i : i + 6].reshape(rows, depth) for i in range(3)], axis=1)
        left, centre, right = [
            dot_nn(tall, conv_w[:, dl].reshape(3 * depth, width)) for dl in range(3)
        ]
        total = centre + pltpu.roll(left, 1, 0) + pltpu.roll(right, rows - 1, 0)
        shape = (6, CTX_COLS, width)
        row_place = wide * half_rows - 1 + iota(shape, 0)
        col_place = narrow * half_cols - 8 + iota(shape, 1)
        inside = (
            (row_place >= 0)
            & (row_place < wide_count * half_rows)
            & (col_place >= 0)
            & (col_place < narrow_count * half_cols)
        )
        features = jnp.where(inside.reshape(rows, width), total, 0.0).astype(BF16)
        res[b] = res[b] + dot_nn(up[...], features).reshape(res.shape[1:])

    def windows(b, part):
        per_part = GROUP_BATCH
        places = []
        for i in range(per_part):
            turn = part * per_part + i
            places.append(lax.rem(narrow + lax.rem(turn, 4) * 2 + turn // 4, WIN))
        before = jnp.concatenate([res[b, :, place].reshape(CELLS, width) for place in places], axis=0)
        normed = layer_norm(before).astype(BF16)
        heads = attend(normed, window_qkv, value_t, bias, 0)
        after = before + dot_nn(heads, window_out[...])
        normed = layer_norm(after).reshape(per_part, WIN, WIN, width)
        for i, place in enumerate(places):
            sent[b, place] = jnp.concatenate(
                [normed[i, :, :, : width // 2], normed[i, :, :, width // 2 :]], axis=1
            ).astype(BF16)
            for j in range(WIN):
                row = lax.rem(my_row + j, WIN)
                target = row * WIN + place
                away = pltpu.make_async_remote_copy(
                    src_ref=sent.at[b, place, row],
                    dst_ref=received.at[b, me],
                    send_sem=there_send.at[b],
                    recv_sem=there_recv.at[b],
                    device_id=device(target),
                    device_id_type=MESH,
                )
                if i or j:
                    away.start()
                else:
                    stays = pltpu.make_async_copy(
                        sent.at[b, place, row], received.at[b, me], there_recv.at[b]
                    )
                    pl.when(target == me)(stays.start)
                    pl.when(target != me)(away.start)
        for i, place in enumerate(places):
            res[b, :, place] = after[i * CELLS : (i + 1) * CELLS].reshape(WIN, WIN, width)

    def sample(b, carry):
        convolve(b)

        def part(half, carry):
            windows(b, half)
            return carry

        lax.fori_loop(0, WIN // GROUP_BATCH, part, 0)
        return carry

    lax.fori_loop(0, batch, sample, 0)

    out_row = iota((256, 256), 0)
    in_row = iota((256, 256), 1)
    perm[0] = jnp.where(
        in_row == (out_row & 15) * 16 + (out_row >> 7) * 8 + ((out_row >> 4) & 7), 1.0, 0.0
    ).astype(BF16)
    perm[1] = jnp.where(
        out_row == (in_row & 15) * 16 + (in_row >> 7) * 8 + ((in_row >> 4) & 7), 1.0, 0.0
    ).astype(BF16)
    fill_bias(grid_table[...], 1, spread, steps, bias)
    loads[4].wait()
    value_t[1] = dot_nt(identity(width), grid_qkv[:, 2 * width :]).astype(BF16)

    def grid(b, carry):
        pltpu.make_async_copy(received.at[b], received.at[b], there_recv.at[b]).wait()
        half_width = width // 2
        for chunk in range(4):
            rows = received[b, chunk * 16 : (chunk + 1) * 16].reshape(256, half_width)
            turned = dot_nn(perm[0], rows).astype(BF16)
            for half in range(2):
                grouped[:, chunk * 16 : (chunk + 1) * 16, half * half_width : (half + 1) * half_width] = (
                    turned[half * 128 : (half + 1) * 128].reshape(WIN, 16, half_width)
                )

        def groups(part, carry):
            start = part * 4
            x = grouped[pl.ds(start, 4)].reshape(4 * CELLS, width)
            heads = attend(x, grid_qkv, value_t, bias, 1)
            heads_buf[pl.ds(start, 4)] = heads.reshape(4, CELLS, width)
            return carry

        lax.fori_loop(0, 2, groups, 0)
        for turn in range(4):
            chunk = lax.rem(me // 16 + turn, 4)
            cut = pl.ds(pl.multiple_of(chunk * 16, 16), 16)
            rows = jnp.concatenate(
                [
                    heads_buf[:, cut, half * half_width : (half + 1) * half_width].reshape(
                        128, half_width
                    )
                    for half in range(2)
                ],
                axis=0,
            )
            answers[b, cut] = dot_nn(perm[1], rows).astype(BF16).reshape(16, 16, half_width)
            for i in range(16):
                target = chunk * 16 + lax.rem(me + i, 16)
                if turn or i:
                    pltpu.make_async_remote_copy(
                        src_ref=answers.at[b, target],
                        dst_ref=returned.at[b, me],
                        send_sem=back_send.at[b],
                        recv_sem=back_recv.at[b],
                        device_id=device(target),
                        device_id_type=MESH,
                    ).start()
                else:
                    pltpu.make_async_copy(
                        answers.at[b, me], returned.at[b, me], back_recv.at[b]
                    ).start()
        return carry

    lax.fori_loop(0, batch, grid, 0)
    loads[5].wait()
    loads[6].wait()
    loads[7].wait()
    gain = gain_ref[...]

    def mlp(step, carry):
        b, half = step // 2, lax.rem(step, 2)

        @pl.when(half == 0)
        def _():
            pltpu.make_async_copy(returned.at[b], returned.at[b], back_recv.at[b]).wait()

        packed = returned[b, pl.ds(pl.multiple_of(half * 32, 32), 32)].astype(F32)
        heads = jnp.concatenate([packed[:, :8], packed[:, 8:]], axis=2)
        heads = heads.reshape(4 * CELLS, width).astype(BF16)
        start = half * 4
        total = res[b, pl.ds(start, 4)].reshape(4 * CELLS, width) + dot_nn(heads, grid_out[...])
        normed = (layer_norm(total) * gain).astype(BF16)
        cut = 512
        for i in range(mlp_in.shape[1] // cut):
            inner = dot_nn(normed, mlp_in[:, i * cut : (i + 1) * cut])
            cubic = inner + 0.044715 * (inner * inner * inner)
            hidden = 0.5 * inner * (1.0 + jnp.tanh(math.sqrt(2.0 / math.pi) * cubic))
            total = total + dot_nn(hidden.astype(BF16), mlp_out[i * cut : (i + 1) * cut, :])
        res[b, pl.ds(start, 4)] = total.reshape(4, WIN, WIN, width)
        pltpu.make_async_copy(
            res.at[b, pl.ds(start, 4)], out_ref.at[b, pl.ds(start, 4)], out_sem
        ).start()
        return carry

    lax.fori_loop(0, 2 * batch, mlp, 0)
    for dw, dn in edges:
        pl.when(exists(dw, dn))(edge_copy(dw, dn).wait_send)
    for b in range(batch):
        for dw in (-1, 1):
            pl.when(exists(dw, 0))(row_copy(b, dw).wait_send)
    for b in range(batch):
        part = received.at[b, pl.ds(0, CELLS - 1)]
        pltpu.make_async_copy(part, part, there_send.at[b]).wait()
        pltpu.make_async_copy(part, part, back_send.at[b]).wait()
    pltpu.make_async_copy(res, out_ref, out_sem).wait()


def on_device(
    latent,
    context,
    conv_weight,
    window_qkv,
    window_out,
    window_bias,
    grid_qkv,
    grid_out,
    grid_bias,
    mlp_gain,
    mlp_in,
    mlp_out,
):
    samples, row_count, col_count, channels = latent.shape
    tiles = latent.reshape(samples, row_count, col_count // WIN, WIN, channels)
    vmem = pltpu.VMEM
    dma = pltpu.SemaphoreType.DMA
    any_spec = pl.BlockSpec(memory_space=pl.ANY)
    vmem_spec = pl.BlockSpec(memory_space=pltpu.VMEM)
    slots = (samples, CELLS, 2 * WIN, channels // 2)
    result = pl.pallas_call(
        block_kernel,
        out_shape=jax.ShapeDtypeStruct(tiles.shape, F32),
        in_specs=[any_spec] * 9 + [vmem_spec] * 3,
        out_specs=any_spec,
        scratch_shapes=[
            vmem(tiles.shape, F32),
            vmem((samples, 8, 32, context.shape[3]), BF16),
            vmem((2, 16, context.shape[3]), BF16),
            vmem((2, 3, 16, context.shape[3]), BF16),
            vmem(conv_weight.shape, BF16),
            vmem(window_qkv.shape, BF16),
            vmem(window_out.shape, BF16),
            vmem(grid_qkv.shape, BF16),
            vmem(grid_out.shape, BF16),
            vmem(mlp_in.shape, BF16),
            vmem(mlp_out.shape, BF16),
            vmem((2, channels, channels), BF16),
            vmem((row_count * col_count, 6 * CTX_COLS), BF16),
            vmem((2, 4, CELLS, 256), F32),
            vmem((240, 1024), F32),
            vmem((15, 8, 1024), F32),
            vmem((2, 256, 256), BF16),
            vmem((samples, WIN, WIN, 2 * WIN, channels // 2), BF16),
            vmem(slots, BF16),
            vmem(slots, BF16),
            vmem(slots, BF16),
            vmem((WIN, CELLS, channels), BF16),
            vmem((WIN, CELLS, channels), BF16),
            dma((8,)),
            dma,
            dma((samples, 2)),
            dma((samples, 2)),
            dma((2, 3)),
            dma((2, 3)),
            dma((samples,)),
            dma((samples,)),
            dma((samples,)),
            dma((samples,)),
            dma,
        ],
        compiler_params=pltpu.CompilerParams(
            collective_id=0, has_side_effects=True, vmem_limit_bytes=56 * 2**20
        ),
        cost_estimate=pl.CostEstimate(
            flops=10_000_000_000, bytes_accessed=16_000_000, transcendentals=4_000_000
        ),
    )(
        tiles,
        context,
        conv_weight,
        window_qkv,
        window_out,
        grid_qkv,
        grid_out,
        mlp_in,
        mlp_out,
        window_bias.transpose(1, 0, 2),
        grid_bias.transpose(1, 0, 2),
        mlp_gain.reshape(1, channels),
    )
    return result.reshape(latent.shape)


def solution(mesh):
    return jax.shard_map(
        on_device,
        mesh=mesh,
        in_specs=(
            P(None, "wide", "narrow", None),
            P(None, "wide", "narrow", None),
            P(),
            P(),
            P(),
            P(),
            P(),
            P(),
            P(),
            P(),
            P(),
            P(),
        ),
        out_specs=P(None, "wide", "narrow", None),
        check_vma=False,
    )
```

```python
import math

import jax
import jax.numpy as jnp
from jax import lax
from jax.experimental import pallas as pl
from jax.experimental.pallas import tpu as pltpu
from jax.sharding import PartitionSpec as P

MESH = pl.DeviceIdType.MESH
F32 = jnp.float32
BF16 = jnp.bfloat16
NORM_EPS = 1e-05
HEAD = 32
WIN = 8
CELLS = WIN * WIN
LOG2E = 1.4426950408889634
CTX_COLS = 48
GROUP_BATCH = 4


def iota(shape, dim):
    return lax.broadcasted_iota(jnp.int32, shape, dim)


def dot_nn(a, b):
    return jnp.dot(a, b, preferred_element_type=F32)


def dot_nt(a, b):
    return lax.dot_general(a, b, (((1,), (1,)), ((), ())), preferred_element_type=F32)


def layer_norm(values):
    center = values - jnp.mean(values, axis=-1, keepdims=True)
    spread = jnp.mean(center * center, axis=-1, keepdims=True)
    return center * lax.rsqrt(spread + NORM_EPS)


def identity(size):
    return jnp.where(iota((size, size), 0) == iota((size, size), 1), 1.0, 0.0).astype(BF16)


def fill_upsampler(up_ref):
    rows, depth = up_ref.shape
    lane = iota((1, depth), 1)
    coarse_row = jnp.zeros((1, depth), jnp.int32)
    for step in range(1, depth // CTX_COLS):
        coarse_row = coarse_row + jnp.where(lane >= step * CTX_COLS, 1, 0)
    coarse_col = lane - coarse_row * CTX_COLS
    block = 64
    for start in range(0, rows, block):
        fine_row = start // 64
        row_centre = fine_row // 2 + 1
        row_other = fine_row // 2 + (2 if fine_row % 2 else 0)
        row_weight = jnp.where(coarse_row == row_centre, 0.75, 0.0) + jnp.where(
            coarse_row == row_other, 0.25, 0.0
        )
        fine_col = iota((block, depth), 0)
        col_centre = (fine_col >> 1) + 8
        col_other = col_centre + 2 * (fine_col & 1) - 1
        col_weight = jnp.where(coarse_col == col_centre, 0.75, 0.0) + jnp.where(
            coarse_col == col_other, 0.25, 0.0
        )
        up_ref[pl.ds(start, block), :] = (row_weight * col_weight).astype(BF16)


def three_terms(values):
    high = values.astype(BF16)
    rest = values - high.astype(F32)
    middle = rest.astype(BF16)
    return high, middle, (rest - middle.astype(F32)).astype(BF16)


def fill_bias(table, which, spread_ref, step_ref, bias_ref):
    turn = jnp.where(iota((16, 15), 0) == iota((16, 15), 1), 1.0, 0.0).astype(BF16)
    pick = jnp.where((iota((240, 1024), 0) & 15) == (iota((240, 1024), 1) >> 6), 1.0, 0.0)
    pick = pick.astype(BF16)
    step_of_lane = iota((16, 240), 1) >> 4
    total = jnp.zeros((240, 1024), F32)
    for term in three_terms(table.reshape(240, 15)):
        turned = dot_nt(turn, term)
        apart = [jnp.where(step_of_lane == a, turned, 0.0).astype(BF16) for a in range(15)]
        total = total + dot_nn(jnp.concatenate(apart, axis=0), pick)
    spread_ref[...] = total * LOG2E
    col_step = (iota((8, 1024), 1) & 7) - iota((8, 1024), 0) + 7

    def one_row_step(a, carry):
        rows = spread_ref[pl.ds(pl.multiple_of(a * 16, 16), 16), :]
        total = jnp.zeros((8, 1024), F32)
        for j in range(15):
            total = jnp.where(col_step == j, jnp.broadcast_to(rows[j : j + 1], (8, 1024)), total)
        step_ref[a] = total
        return carry

    lax.fori_loop(0, 15, one_row_step, 0)
    query_row = (iota((8, 1024), 1) >> 3) & 7

    def one_key_row(rq, carry):
        total = jnp.zeros((8, 1024), F32)
        for rp in range(8):
            total = jnp.where(query_row == rp, step_ref[rp - rq + 7], total)
        for block in range(4):
            bias_ref[which, block, pl.ds(pl.multiple_of(rq * 8, 8), 8), :] = total[
                :, block * 256 : (block + 1) * 256
            ]
        return carry

    lax.fori_loop(0, 8, one_key_row, 0)


def attend(x, qkv_ref, value_ref, bias_ref, which):
    width = x.shape[1]
    count = x.shape[0] // CELLS
    queries = dot_nn(x, qkv_ref[:, 0:width]).astype(BF16)
    keys = dot_nn(x, qkv_ref[:, width : 2 * width]).astype(BF16)
    values = dot_nt(value_ref[which], x).astype(BF16)
    head_of_lane = iota((CELLS, 128), 1) >> 5
    head_masks = [jnp.where(head_of_lane == h, 1.0, 0.0).astype(BF16) for h in range(4)]
    group_of_lane = iota((128, count * CELLS), 1) >> 6
    group_masks = [jnp.where(group_of_lane == g, 1.0, 0.0).astype(BF16) for g in range(count)]
    low = iota((HEAD, 128), 1) < 64
    outs = []
    for block in range(width // 128):
        lanes = slice(block * 128, (block + 1) * 128)
        bias = bias_ref[which, block]
        weights = []
        for g in range(count):
            rows = slice(g * CELLS, (g + 1) * CELLS)
            query = queries[rows, lanes]
            spread = jnp.concatenate([query * mask for mask in head_masks], axis=0)
            scores = dot_nt(keys[rows, lanes], spread) * (LOG2E * HEAD**-0.5) + bias
            lifted = jnp.exp2(scores - jnp.max(scores, axis=0, keepdims=True))
            inverse = 1.0 / jnp.sum(lifted, axis=0, keepdims=True)
            weights.append((lifted * inverse).astype(BF16))
        weight = jnp.concatenate(weights, axis=0)
        value = values[lanes]
        stacked = jnp.concatenate([value * mask for mask in group_masks], axis=0)
        blended = dot_nn(stacked, weight)
        for h in range(4):
            picked = []
            for pair in range(count // 2):
                parts = []
                for g in (2 * pair, 2 * pair + 1):
                    parts.append(
                        blended[
                            g * 128 + h * HEAD : g * 128 + (h + 1) * HEAD,
                            (h // 2) * 128 : (h // 2 + 1) * 128,
                        ]
                    )
                first, second = parts
                if h % 2 == 0:
                    picked.append(jnp.where(low, first, pltpu.roll(second, 64, 1)))
                else:
                    picked.append(jnp.where(low, pltpu.roll(first, 64, 1), second))
            outs.append(jnp.concatenate(picked, axis=1).astype(BF16))
    turned = jnp.concatenate(outs, axis=0)
    return dot_nt(identity(count * CELLS), turned).astype(BF16)


def block_kernel(
    latent_ref,
    context_ref,
    conv_hbm,
    window_qkv_hbm,
    window_out_hbm,
    grid_qkv_hbm,
    grid_out_hbm,
    mlp_in_hbm,
    mlp_out_hbm,
    window_table,
    grid_table,
    gain_ref,
    out_ref,
    res,
    halo,
    edge_out,
    edge_in,
    conv_w,
    window_qkv,
    window_out,
    grid_qkv,
    grid_out,
    mlp_in,
    mlp_out,
    value_t,
    up,
    bias,
    spread,
    steps,
    perm,
    sent,
    received,
    answers,
    returned,
    grouped,
    heads_buf,
    load_sem,
    own_sem,
    row_send,
    row_recv,
    edge_send,
    edge_recv,
    there_send,
    there_recv,
    back_send,
    back_recv,
    out_sem,
):
    wide = lax.axis_index("wide")
    narrow = lax.axis_index("narrow")
    wide_count = lax.axis_size("wide")
    narrow_count = lax.axis_size("narrow")
    planes = wide_count // WIN
    plane = lax.rem(wide, planes)
    my_row = wide // planes
    me = my_row * WIN + narrow

    def device(place):
        return ((place // WIN) * planes + plane, lax.rem(place, WIN))

    loads = [
        pltpu.make_async_copy(source, target, load_sem.at[i])
        for i, (source, target) in enumerate(
            (
                (conv_hbm, conv_w),
                (latent_ref, res),
                (window_qkv_hbm, window_qkv),
                (window_out_hbm, window_out),
                (grid_qkv_hbm, grid_qkv),
                (grid_out_hbm, grid_out),
                (mlp_in_hbm, mlp_in),
                (mlp_out_hbm, mlp_out),
            )
        )
    ]
    half_rows, half_cols = context_ref.shape[1], context_ref.shape[2]
    depth = context_ref.shape[3]
    batch = latent_ref.shape[0]
    own = pltpu.make_async_copy(context_ref, halo.at[:, pl.ds(2, half_rows)], own_sem)
    own.start()
    edge_in[...] = jnp.zeros_like(edge_in)

    barrier = pltpu.get_barrier_semaphore()

    def greet(i, carry):
        pl.semaphore_signal(
            barrier, inc=1, device_id=device(lax.rem(me + i, CELLS)), device_id_type=MESH
        )
        return carry

    def neighbour(dw, dn):
        return (
            lax.rem(wide + dw + wide_count, wide_count),
            lax.rem(narrow + dn + narrow_count, narrow_count),
        )

    for dw in (-1, 1):
        for dn in (0, -1, 1):
            pl.semaphore_signal(barrier, inc=1, device_id=neighbour(dw, dn), device_id_type=MESH)
    for i in (CELLS - 1, *range(1, CELLS - 1)):
        greet(i, 0)
    for load in loads[:4]:
        load.start()

    own.wait()
    pl.semaphore_wait(barrier, CELLS - 1 + 6)

    def exists(dw, dn):
        return (
            (wide + dw >= 0)
            & (wide + dw < wide_count)
            & (narrow + dn >= 0)
            & (narrow + dn < narrow_count)
        )

    def row_copy(b, dw):
        lane = (dw + 1) // 2
        return pltpu.make_async_remote_copy(
            src_ref=halo.at[b, pl.ds(half_rows if dw > 0 else 2, 2)],
            dst_ref=halo.at[b, pl.ds(0 if dw > 0 else half_rows + 2, 2)],
            send_sem=row_send.at[b, lane],
            recv_sem=row_recv.at[b, lane],
            device_id=neighbour(dw, 0),
            device_id_type=MESH,
        )

    def edge_copy(dw, dn):
        side = (dn + 1) // 2
        return pltpu.make_async_remote_copy(
            src_ref=edge_out.at[side],
            dst_ref=edge_in.at[1 - side, 1 - dw],
            send_sem=edge_send.at[side, 1 - dw],
            recv_sem=edge_recv.at[1 - side, 1 - dw],
            device_id=neighbour(dw, dn),
            device_id_type=MESH,
        )

    edges = [(dw, dn) for dn in (-1, 1) for dw in (-1, 0, 1)]
    for dw in (-1, 1):
        pl.when(exists(dw, 0))(row_copy(0, dw).start)
    for side in range(2):
        strip = halo[:, 2 : 2 + half_rows, side * 16 : side * 16 + 16, :].reshape(
            batch * half_rows * 16, depth
        )
        row = iota((16, batch * half_rows * 16), 0)
        pick = iota((16, batch * half_rows * 16), 1) == (row >> 1) * 16 + (row & 1) + 14 * side
        edge_out[side] = dot_nn(jnp.where(pick, 1.0, 0.0).astype(BF16), strip).astype(BF16)
    for dw, dn in edges:
        pl.when(exists(dw, dn))(edge_copy(dw, dn).start)
    for b in range(1, batch):
        for dw in (-1, 1):
            pl.when(exists(dw, 0))(row_copy(b, dw).start)

    for load in loads[4:]:
        load.start()

    fill_bias(window_table[...], 0, spread, steps, bias)
    fill_upsampler(up)
    width = window_out.shape[0]
    loads[2].wait()
    value_t[0] = dot_nt(identity(width), window_qkv[:, 2 * width :]).astype(BF16)
    for dw, dn in edges:
        pl.when(exists(-dw, -dn))(edge_copy(dw, dn).wait_recv)
    loads[0].wait()
    loads[1].wait()
    loads[3].wait()
    def convolve(b):
        for dw in (-1, 1):
            lane = (dw + 1) // 2
            arrived = halo.at[b, pl.ds(0 if dw > 0 else half_rows + 2, 2)]
            pl.when(exists(-dw, 0))(
                pltpu.make_async_copy(arrived, arrived, row_recv.at[b, lane]).wait
            )
        sides = []
        place, taken = iota((64, 48), 0), iota((64, 48), 1)
        row, col = place >> 3, place & 7
        slot = jnp.where(row < 2, 0, jnp.where(row < 2 + half_rows, 1, 2))
        their_row = jnp.where(row < 2, row + half_rows - 2, row - 2)
        their_row = jnp.where(row < 2 + half_rows, their_row, row - 2 - half_rows)
        base = slot * 16 + b * (2 * half_rows) + their_row * 2
        for side in range(2):
            first = 6 if side == 0 else 0
            chosen = (taken == base + col - first) & (col >= first) & (col < first + 2)
            strip = dot_nn(
                jnp.where(chosen, 1.0, 0.0).astype(BF16), edge_in[side].reshape(48, depth)
            )
            sides.append(strip.reshape(8, 8, depth))
        widened = jnp.concatenate([sides[0], halo[b].astype(F32), sides[1]], axis=1)
        shape = (8, CTX_COLS, depth)
        row_place = wide * half_rows - 2 + iota(shape, 0)
        col_place = narrow * half_cols - 8 + iota(shape, 1)
        inside = (
            (row_place >= 0)
            & (row_place < wide_count * half_rows)
            & (col_place >= 0)
            & (col_place < narrow_count * half_cols)
        )
        widened = jnp.where(inside, widened, 0.0).astype(BF16)
        rows = 6 * CTX_COLS
        tall = jnp.concatenate([widened[i : i + 6].reshape(rows, depth) for i in range(3)], axis=1)
        left, centre, right = [
            dot_nn(tall, conv_w[:, dl].reshape(3 * depth, width)) for dl in range(3)
        ]
        total = centre + pltpu.roll(left, 1, 0) + pltpu.roll(right, rows - 1, 0)
        shape = (6, CTX_COLS, width)
        row_place = wide * half_rows - 1 + iota(shape, 0)
        col_place = narrow * half_cols - 8 + iota(shape, 1)
        inside = (
            (row_place >= 0)
            & (row_place < wide_count * half_rows)
            & (col_place >= 0)
            & (col_place < narrow_count * half_cols)
        )
        features = jnp.where(inside.reshape(rows, width), total, 0.0).astype(BF16)
        res[b] = res[b] + dot_nn(up[...], features).reshape(res.shape[1:])

    def windows(b, part):
        per_part = GROUP_BATCH
        places = []
        for i in range(per_part):
            turn = part * per_part + i
            places.append(lax.rem(narrow + lax.rem(turn, 4) * 2 + turn // 4, WIN))
        before = jnp.concatenate([res[b, :, place].reshape(CELLS, width) for place in places], axis=0)
        normed = layer_norm(before).astype(BF16)
        heads = attend(normed, window_qkv, value_t, bias, 0)
        after = before + dot_nn(heads, window_out[...])
        normed = layer_norm(after).reshape(per_part, WIN, WIN, width)
        for i, place in enumerate(places):
            sent[b, place] = jnp.concatenate(
                [normed[i, :, :, : width // 2], normed[i, :, :, width // 2 :]], axis=1
            ).astype(BF16)
            for j in range(WIN):
                row = lax.rem(my_row + j, WIN)
                target = row * WIN + place
                away = pltpu.make_async_remote_copy(
                    src_ref=sent.at[b, place, row],
                    dst_ref=received.at[b, me],
                    send_sem=there_send.at[b],
                    recv_sem=there_recv.at[b],
                    device_id=device(target),
                    device_id_type=MESH,
                )
                if i or j:
                    away.start()
                else:
                    stays = pltpu.make_async_copy(
                        sent.at[b, place, row], received.at[b, me], there_recv.at[b]
                    )
                    pl.when(target == me)(stays.start)
                    pl.when(target != me)(away.start)
        for i, place in enumerate(places):
            res[b, :, place] = after[i * CELLS : (i + 1) * CELLS].reshape(WIN, WIN, width)

    def sample(b, carry):
        convolve(b)

        def part(half, carry):
            windows(b, half)
            return carry

        lax.fori_loop(0, WIN // GROUP_BATCH, part, 0)
        return carry

    lax.fori_loop(0, batch, sample, 0)

    out_row = iota((256, 256), 0)
    in_row = iota((256, 256), 1)
    perm[0] = jnp.where(
        in_row == (out_row & 15) * 16 + (out_row >> 7) * 8 + ((out_row >> 4) & 7), 1.0, 0.0
    ).astype(BF16)
    perm[1] = jnp.where(
        out_row == (in_row & 15) * 16 + (in_row >> 7) * 8 + ((in_row >> 4) & 7), 1.0, 0.0
    ).astype(BF16)
    fill_bias(grid_table[...], 1, spread, steps, bias)
    loads[4].wait()
    value_t[1] = dot_nt(identity(width), grid_qkv[:, 2 * width :]).astype(BF16)

    def grid(b, carry):
        pltpu.make_async_copy(received.at[b], received.at[b], there_recv.at[b]).wait()
        half_width = width // 2
        for chunk in range(4):
            rows = received[b, chunk * 16 : (chunk + 1) * 16].reshape(256, half_width)
            turned = dot_nn(perm[0], rows).astype(BF16)
            for half in range(2):
                grouped[:, chunk * 16 : (chunk + 1) * 16, half * half_width : (half + 1) * half_width] = (
                    turned[half * 128 : (half + 1) * 128].reshape(WIN, 16, half_width)
                )

        def groups(part, carry):
            start = part * 4
            x = grouped[pl.ds(start, 4)].reshape(4 * CELLS, width)
            heads = attend(x, grid_qkv, value_t, bias, 1)
            heads_buf[pl.ds(start, 4)] = heads.reshape(4, CELLS, width)
            return carry

        lax.fori_loop(0, 2, groups, 0)
        for turn in range(4):
            chunk = lax.rem(me // 16 + turn, 4)
            cut = pl.ds(pl.multiple_of(chunk * 16, 16), 16)
            rows = jnp.concatenate(
                [
                    heads_buf[:, cut, half * half_width : (half + 1) * half_width].reshape(
                        128, half_width
                    )
                    for half in range(2)
                ],
                axis=0,
            )
            answers[b, cut] = dot_nn(perm[1], rows).astype(BF16).reshape(16, 16, half_width)
            for i in range(16):
                target = chunk * 16 + lax.rem(me + i, 16)
                if turn or i:
                    pltpu.make_async_remote_copy(
                        src_ref=answers.at[b, target],
                        dst_ref=returned.at[b, me],
                        send_sem=back_send.at[b],
                        recv_sem=back_recv.at[b],
                        device_id=device(target),
                        device_id_type=MESH,
                    ).start()
                else:
                    pltpu.make_async_copy(
                        answers.at[b, me], returned.at[b, me], back_recv.at[b]
                    ).start()
        return carry

    lax.fori_loop(0, batch, grid, 0)
    loads[5].wait()
    loads[6].wait()
    loads[7].wait()
    gain = gain_ref[...]

    def mlp(step, carry):
        b = step
        pltpu.make_async_copy(returned.at[b], returned.at[b], back_recv.at[b]).wait()
        packed = returned[b].astype(F32)
        heads = jnp.concatenate([packed[:, :8], packed[:, 8:]], axis=2)
        heads = heads.reshape(8 * CELLS, width).astype(BF16)
        start = 0
        total = res[b].reshape(8 * CELLS, width) + dot_nn(heads, grid_out[...])
        normed = (layer_norm(total) * gain).astype(BF16)
        cut = 256
        for i in range(mlp_in.shape[1] // cut):
            inner = dot_nn(normed, mlp_in[:, i * cut : (i + 1) * cut])
            cubic = inner + 0.044715 * (inner * inner * inner)
            hidden = 0.5 * inner * (1.0 + jnp.tanh(math.sqrt(2.0 / math.pi) * cubic))
            total = total + dot_nn(hidden.astype(BF16), mlp_out[i * cut : (i + 1) * cut, :])
        res[b] = total.reshape(8, WIN, WIN, width)
        pltpu.make_async_copy(
            res.at[b], out_ref.at[b], out_sem
        ).start()
        return carry

    lax.fori_loop(0, batch, mlp, 0)
    for dw, dn in edges:
        pl.when(exists(dw, dn))(edge_copy(dw, dn).wait_send)
    for b in range(batch):
        for dw in (-1, 1):
            pl.when(exists(dw, 0))(row_copy(b, dw).wait_send)
    for b in range(batch):
        part = received.at[b, pl.ds(0, CELLS - 1)]
        pltpu.make_async_copy(part, part, there_send.at[b]).wait()
        pltpu.make_async_copy(part, part, back_send.at[b]).wait()
    pltpu.make_async_copy(res, out_ref, out_sem).wait()


def copy_kernel(source_ref, target_ref, held, in_sem, out_sem):
    batch, rows = held.shape[0], held.shape[1]
    pieces = [(b, pl.ds(row, 2)) for b in range(batch) for row in range(0, rows, 2)]
    loads = [
        pltpu.make_async_copy(source_ref.at[piece], held.at[piece], in_sem.at[i])
        for i, piece in enumerate(pieces)
    ]
    stores = [
        pltpu.make_async_copy(held.at[piece], target_ref.at[piece], out_sem.at[i])
        for i, piece in enumerate(pieces)
    ]
    for load in loads:
        load.start()
    for load, store in zip(loads, stores):
        load.wait()
        store.start()
    for store in stores:
        store.wait()


def on_device(
    latent,
    context,
    conv_weight,
    window_qkv,
    window_out,
    window_bias,
    grid_qkv,
    grid_out,
    grid_bias,
    mlp_gain,
    mlp_in,
    mlp_out,
):
    samples, row_count, col_count, channels = latent.shape
    tiles = latent.reshape(samples, row_count, col_count // WIN, WIN, channels)
    vmem = pltpu.VMEM
    dma = pltpu.SemaphoreType.DMA
    any_spec = pl.BlockSpec(memory_space=pl.ANY)
    vmem_spec = pl.BlockSpec(memory_space=pltpu.VMEM)
    slots = (samples, CELLS, 2 * WIN, channels // 2)
    result = pl.pallas_call(
        block_kernel,
        out_shape=jax.ShapeDtypeStruct(tiles.shape, F32),
        in_specs=[any_spec] * 9 + [vmem_spec] * 3,
        out_specs=any_spec,
        scratch_shapes=[
            vmem(tiles.shape, F32),
            vmem((samples, 8, 32, context.shape[3]), BF16),
            vmem((2, 16, context.shape[3]), BF16),
            vmem((2, 3, 16, context.shape[3]), BF16),
            vmem(conv_weight.shape, BF16),
            vmem(window_qkv.shape, BF16),
            vmem(window_out.shape, BF16),
            vmem(grid_qkv.shape, BF16),
            vmem(grid_out.shape, BF16),
            vmem(mlp_in.shape, BF16),
            vmem(mlp_out.shape, BF16),
            vmem((2, channels, channels), BF16),
            vmem((row_count * col_count, 6 * CTX_COLS), BF16),
            vmem((2, 4, CELLS, 256), F32),
            vmem((240, 1024), F32),
            vmem((15, 8, 1024), F32),
            vmem((2, 256, 256), BF16),
            vmem((samples, WIN, WIN, 2 * WIN, channels // 2), BF16),
            vmem(slots, BF16),
            vmem(slots, BF16),
            vmem(slots, BF16),
            vmem((WIN, CELLS, channels), BF16),
            vmem((WIN, CELLS, channels), BF16),
            dma((8,)),
            dma,
            dma((samples, 2)),
            dma((samples, 2)),
            dma((2, 3)),
            dma((2, 3)),
            dma((samples,)),
            dma((samples,)),
            dma((samples,)),
            dma((samples,)),
            dma,
        ],
        compiler_params=pltpu.CompilerParams(
            collective_id=0, has_side_effects=True, vmem_limit_bytes=56 * 2**20
        ),
        cost_estimate=pl.CostEstimate(
            flops=10_000_000_000, bytes_accessed=16_000_000, transcendentals=4_000_000
        ),
    )(
        tiles,
        context,
        conv_weight,
        window_qkv,
        window_out,
        grid_qkv,
        grid_out,
        mlp_in,
        mlp_out,
        window_bias.transpose(1, 0, 2),
        grid_bias.transpose(1, 0, 2),
        mlp_gain.reshape(1, channels),
    )
    result = pl.pallas_call(
        copy_kernel,
        out_shape=jax.ShapeDtypeStruct(tiles.shape, F32),
        in_specs=[any_spec],
        out_specs=any_spec,
        scratch_shapes=[vmem(tiles.shape, F32), dma((4 * samples,)), dma((4 * samples,))],
        compiler_params=pltpu.CompilerParams(vmem_limit_bytes=56 * 2**20),
    )(result)
    return result.reshape(latent.shape)


def solution(mesh):
    return jax.shard_map(
        on_device,
        mesh=mesh,
        in_specs=(
            P(None, "wide", "narrow", None),
            P(None, "wide", "narrow", None),
            P(),
            P(),
            P(),
            P(),
            P(),
            P(),
            P(),
            P(),
            P(),
            P(),
        ),
        out_specs=P(None, "wide", "narrow", None),
        check_vma=False,
    )
```

```python
import math

import jax
import jax.numpy as jnp
from jax import lax
from jax.experimental import pallas as pl
from jax.experimental.pallas import tpu as pltpu
from jax.sharding import PartitionSpec as P

MESH = pl.DeviceIdType.MESH
F32 = jnp.float32
BF16 = jnp.bfloat16
NORM_EPS = 1e-05
HEAD = 32
WIN = 8
CELLS = WIN * WIN
LOG2E = 1.4426950408889634
CTX_COLS = 48
GROUP_BATCH = 4


def iota(shape, dim):
    return lax.broadcasted_iota(jnp.int32, shape, dim)


def dot_nn(a, b):
    return jnp.dot(a, b, preferred_element_type=F32)


def dot_nt(a, b):
    return lax.dot_general(a, b, (((1,), (1,)), ((), ())), preferred_element_type=F32)


def layer_norm(values):
    center = values - jnp.mean(values, axis=-1, keepdims=True)
    spread = jnp.mean(center * center, axis=-1, keepdims=True)
    return center * lax.rsqrt(spread + NORM_EPS)


def identity(size):
    return jnp.where(iota((size, size), 0) == iota((size, size), 1), 1.0, 0.0).astype(BF16)


def fill_upsampler(up_ref):
    rows, depth = up_ref.shape
    lane = iota((1, depth), 1)
    coarse_row = jnp.zeros((1, depth), jnp.int32)
    for step in range(1, depth // CTX_COLS):
        coarse_row = coarse_row + jnp.where(lane >= step * CTX_COLS, 1, 0)
    coarse_col = lane - coarse_row * CTX_COLS
    block = 64
    for start in range(0, rows, block):
        fine_row = start // 64
        row_centre = fine_row // 2 + 1
        row_other = fine_row // 2 + (2 if fine_row % 2 else 0)
        row_weight = jnp.where(coarse_row == row_centre, 0.75, 0.0) + jnp.where(
            coarse_row == row_other, 0.25, 0.0
        )
        fine_col = iota((block, depth), 0)
        col_centre = (fine_col >> 1) + 8
        col_other = col_centre + 2 * (fine_col & 1) - 1
        col_weight = jnp.where(coarse_col == col_centre, 0.75, 0.0) + jnp.where(
            coarse_col == col_other, 0.25, 0.0
        )
        up_ref[pl.ds(start, block), :] = (row_weight * col_weight).astype(BF16)


def three_terms(values):
    high = values.astype(BF16)
    rest = values - high.astype(F32)
    middle = rest.astype(BF16)
    return high, middle, (rest - middle.astype(F32)).astype(BF16)


def fill_bias(table, which, spread_ref, step_ref, bias_ref):
    turn = jnp.where(iota((16, 15), 0) == iota((16, 15), 1), 1.0, 0.0).astype(BF16)
    pick = jnp.where((iota((240, 1024), 0) & 15) == (iota((240, 1024), 1) >> 6), 1.0, 0.0)
    pick = pick.astype(BF16)
    step_of_lane = iota((16, 240), 1) >> 4
    total = jnp.zeros((240, 1024), F32)
    for term in three_terms(table.reshape(240, 15)):
        turned = dot_nt(turn, term)
        apart = [jnp.where(step_of_lane == a, turned, 0.0).astype(BF16) for a in range(15)]
        total = total + dot_nn(jnp.concatenate(apart, axis=0), pick)
    spread_ref[...] = total * LOG2E
    col_step = (iota((8, 1024), 1) & 7) - iota((8, 1024), 0) + 7

    def one_row_step(a, carry):
        rows = spread_ref[pl.ds(pl.multiple_of(a * 16, 16), 16), :]
        total = jnp.zeros((8, 1024), F32)
        for j in range(15):
            total = jnp.where(col_step == j, jnp.broadcast_to(rows[j : j + 1], (8, 1024)), total)
        step_ref[a] = total
        return carry

    lax.fori_loop(0, 15, one_row_step, 0)
    query_row = (iota((8, 1024), 1) >> 3) & 7

    def one_key_row(rq, carry):
        total = jnp.zeros((8, 1024), F32)
        for rp in range(8):
            total = jnp.where(query_row == rp, step_ref[rp - rq + 7], total)
        for block in range(4):
            bias_ref[which, block, pl.ds(pl.multiple_of(rq * 8, 8), 8), :] = total[
                :, block * 256 : (block + 1) * 256
            ]
        return carry

    lax.fori_loop(0, 8, one_key_row, 0)


def attend(x, qkv_ref, value_ref, bias_ref, which):
    width = x.shape[1]
    count = x.shape[0] // CELLS
    queries = dot_nn(x, qkv_ref[:, 0:width]).astype(BF16)
    keys = dot_nn(x, qkv_ref[:, width : 2 * width]).astype(BF16)
    values = dot_nt(value_ref[which], x).astype(BF16)
    head_of_lane = iota((CELLS, 128), 1) >> 5
    head_masks = [jnp.where(head_of_lane == h, 1.0, 0.0).astype(BF16) for h in range(4)]
    group_of_lane = iota((128, count * CELLS), 1) >> 6
    group_masks = [jnp.where(group_of_lane == g, 1.0, 0.0).astype(BF16) for g in range(count)]
    low = iota((HEAD, 128), 1) < 64
    outs = []
    for block in range(width // 128):
        lanes = slice(block * 128, (block + 1) * 128)
        bias = bias_ref[which, block]
        weights = []
        for g in range(count):
            rows = slice(g * CELLS, (g + 1) * CELLS)
            query = queries[rows, lanes]
            spread = jnp.concatenate([query * mask for mask in head_masks], axis=0)
            scores = dot_nt(keys[rows, lanes], spread) * (LOG2E * HEAD**-0.5) + bias
            lifted = jnp.exp2(scores - jnp.max(scores, axis=0, keepdims=True))
            inverse = 1.0 / jnp.sum(lifted, axis=0, keepdims=True)
            weights.append((lifted * inverse).astype(BF16))
        weight = jnp.concatenate(weights, axis=0)
        value = values[lanes]
        stacked = jnp.concatenate([value * mask for mask in group_masks], axis=0)
        blended = dot_nn(stacked, weight)
        for h in range(4):
            picked = []
            for pair in range(count // 2):
                parts = []
                for g in (2 * pair, 2 * pair + 1):
                    parts.append(
                        blended[
                            g * 128 + h * HEAD : g * 128 + (h + 1) * HEAD,
                            (h // 2) * 128 : (h // 2 + 1) * 128,
                        ]
                    )
                first, second = parts
                if h % 2 == 0:
                    picked.append(jnp.where(low, first, pltpu.roll(second, 64, 1)))
                else:
                    picked.append(jnp.where(low, pltpu.roll(first, 64, 1), second))
            outs.append(jnp.concatenate(picked, axis=1).astype(BF16))
    turned = jnp.concatenate(outs, axis=0)
    return dot_nt(identity(count * CELLS), turned).astype(BF16)


def block_kernel(
    latent_ref,
    context_ref,
    conv_hbm,
    window_qkv_hbm,
    window_out_hbm,
    grid_qkv_hbm,
    grid_out_hbm,
    mlp_in_hbm,
    mlp_out_hbm,
    window_table,
    grid_table,
    gain_ref,
    out_ref,
    res,
    halo,
    edge_out,
    edge_in,
    conv_w,
    window_qkv,
    window_out,
    grid_qkv,
    grid_out,
    mlp_in,
    mlp_out,
    value_t,
    up,
    bias,
    spread,
    steps,
    perm,
    sent,
    received,
    answers,
    returned,
    grouped,
    heads_buf,
    load_sem,
    own_sem,
    row_send,
    row_recv,
    edge_send,
    edge_recv,
    there_send,
    there_recv,
    back_send,
    back_recv,
    out_sem,
    plane_sem,
):
    wide = lax.axis_index("wide")
    narrow = lax.axis_index("narrow")
    wide_count = lax.axis_size("wide")
    narrow_count = lax.axis_size("narrow")
    planes = wide_count // WIN
    plane = lax.rem(wide, planes)
    my_row = wide // planes
    me = my_row * WIN + narrow

    def device(place):
        return ((place // WIN) * planes + plane, lax.rem(place, WIN))

    loads = [
        pltpu.make_async_copy(source, target, load_sem.at[i])
        for i, (source, target) in enumerate(
            (
                (conv_hbm, conv_w),
                (latent_ref, res),
                (window_qkv_hbm, window_qkv),
                (window_out_hbm, window_out),
                (grid_qkv_hbm, grid_qkv),
                (grid_out_hbm, grid_out),
                (mlp_in_hbm, mlp_in),
                (mlp_out_hbm, mlp_out),
            )
        )
    ]
    half_rows, half_cols = context_ref.shape[1], context_ref.shape[2]
    depth = context_ref.shape[3]
    batch = latent_ref.shape[0]
    own = pltpu.make_async_copy(context_ref, halo.at[:, pl.ds(2, half_rows)], own_sem)
    own.start()
    edge_in[...] = jnp.zeros_like(edge_in)

    barrier = pltpu.get_barrier_semaphore()

    row_peers = [my_row * WIN + lax.rem(narrow + i, WIN) for i in (1, WIN - 1, *range(2, WIN - 1))]
    column_peers = [lax.rem(my_row + i, WIN) * WIN + narrow for i in range(1, WIN)]

    def neighbour(dw, dn):
        return (
            lax.rem(wide + dw + wide_count, wide_count),
            lax.rem(narrow + dn + narrow_count, narrow_count),
        )

    for dw in (-1, 1):
        for dn in (0, -1, 1):
            pl.semaphore_signal(barrier, inc=1, device_id=neighbour(dw, dn), device_id_type=MESH)
    for place in row_peers + column_peers:
        pl.semaphore_signal(barrier, inc=1, device_id=device(place), device_id_type=MESH)
    for load in loads[:4]:
        load.start()

    own.wait()
    pl.semaphore_wait(barrier, 2 * (WIN - 1) + 6)

    def exists(dw, dn):
        return (
            (wide + dw >= 0)
            & (wide + dw < wide_count)
            & (narrow + dn >= 0)
            & (narrow + dn < narrow_count)
        )

    def row_copy(b, dw):
        lane = (dw + 1) // 2
        return pltpu.make_async_remote_copy(
            src_ref=halo.at[b, pl.ds(half_rows if dw > 0 else 2, 2)],
            dst_ref=halo.at[b, pl.ds(0 if dw > 0 else half_rows + 2, 2)],
            send_sem=row_send.at[b, lane],
            recv_sem=row_recv.at[b, lane],
            device_id=neighbour(dw, 0),
            device_id_type=MESH,
        )

    def edge_copy(dw, dn):
        side = (dn + 1) // 2
        return pltpu.make_async_remote_copy(
            src_ref=edge_out.at[side],
            dst_ref=edge_in.at[1 - side, 1 - dw],
            send_sem=edge_send.at[side, 1 - dw],
            recv_sem=edge_recv.at[1 - side, 1 - dw],
            device_id=neighbour(dw, dn),
            device_id_type=MESH,
        )

    edges = [(dw, dn) for dn in (-1, 1) for dw in (-1, 0, 1)]
    for dw in (-1, 1):
        pl.when(exists(dw, 0))(row_copy(0, dw).start)
    for side in range(2):
        strip = halo[:, 2 : 2 + half_rows, side * 16 : side * 16 + 16, :].reshape(
            batch * half_rows * 16, depth
        )
        row = iota((16, batch * half_rows * 16), 0)
        pick = iota((16, batch * half_rows * 16), 1) == (row >> 1) * 16 + (row & 1) + 14 * side
        edge_out[side] = dot_nn(jnp.where(pick, 1.0, 0.0).astype(BF16), strip).astype(BF16)
    for dw, dn in edges:
        pl.when(exists(dw, dn))(edge_copy(dw, dn).start)
    for b in range(1, batch):
        for dw in (-1, 1):
            pl.when(exists(dw, 0))(row_copy(b, dw).start)

    for place in column_peers:
        pl.semaphore_signal(plane_sem, inc=1, device_id=device(place), device_id_type=MESH)
    for load in loads[4:]:
        load.start()

    fill_bias(window_table[...], 0, spread, steps, bias)
    fill_upsampler(up)
    width = window_out.shape[0]
    loads[2].wait()
    value_t[0] = dot_nt(identity(width), window_qkv[:, 2 * width :]).astype(BF16)
    for dw, dn in edges:
        pl.when(exists(-dw, -dn))(edge_copy(dw, dn).wait_recv)
    loads[0].wait()
    loads[1].wait()
    loads[3].wait()
    def convolve(b):
        for dw in (-1, 1):
            lane = (dw + 1) // 2
            arrived = halo.at[b, pl.ds(0 if dw > 0 else half_rows + 2, 2)]
            pl.when(exists(-dw, 0))(
                pltpu.make_async_copy(arrived, arrived, row_recv.at[b, lane]).wait
            )
        sides = []
        place, taken = iota((64, 48), 0), iota((64, 48), 1)
        row, col = place >> 3, place & 7
        slot = jnp.where(row < 2, 0, jnp.where(row < 2 + half_rows, 1, 2))
        their_row = jnp.where(row < 2, row + half_rows - 2, row - 2)
        their_row = jnp.where(row < 2 + half_rows, their_row, row - 2 - half_rows)
        base = slot * 16 + b * (2 * half_rows) + their_row * 2
        for side in range(2):
            first = 6 if side == 0 else 0
            chosen = (taken == base + col - first) & (col >= first) & (col < first + 2)
            strip = dot_nn(
                jnp.where(chosen, 1.0, 0.0).astype(BF16), edge_in[side].reshape(48, depth)
            )
            sides.append(strip.reshape(8, 8, depth))
        widened = jnp.concatenate([sides[0], halo[b].astype(F32), sides[1]], axis=1)
        shape = (8, CTX_COLS, depth)
        row_place = wide * half_rows - 2 + iota(shape, 0)
        col_place = narrow * half_cols - 8 + iota(shape, 1)
        inside = (
            (row_place >= 0)
            & (row_place < wide_count * half_rows)
            & (col_place >= 0)
            & (col_place < narrow_count * half_cols)
        )
        widened = jnp.where(inside, widened, 0.0).astype(BF16)
        rows = 6 * CTX_COLS
        tall = jnp.concatenate([widened[i : i + 6].reshape(rows, depth) for i in range(3)], axis=1)
        left, centre, right = [
            dot_nn(tall, conv_w[:, dl].reshape(3 * depth, width)) for dl in range(3)
        ]
        total = centre + pltpu.roll(left, 1, 0) + pltpu.roll(right, rows - 1, 0)
        shape = (6, CTX_COLS, width)
        row_place = wide * half_rows - 1 + iota(shape, 0)
        col_place = narrow * half_cols - 8 + iota(shape, 1)
        inside = (
            (row_place >= 0)
            & (row_place < wide_count * half_rows)
            & (col_place >= 0)
            & (col_place < narrow_count * half_cols)
        )
        features = jnp.where(inside.reshape(rows, width), total, 0.0).astype(BF16)
        res[b] = res[b] + dot_nn(up[...], features).reshape(res.shape[1:])

    def windows(b, part):
        per_part = GROUP_BATCH
        places = []
        for i in range(per_part):
            turn = part * per_part + i
            places.append(lax.rem(narrow + lax.rem(turn, 4) * 2 + turn // 4, WIN))
        before = jnp.concatenate([res[b, :, place].reshape(CELLS, width) for place in places], axis=0)
        normed = layer_norm(before).astype(BF16)
        heads = attend(normed, window_qkv, value_t, bias, 0)
        after = before + dot_nn(heads, window_out[...])
        normed = layer_norm(after).reshape(per_part, WIN, WIN, width)
        for i, place in enumerate(places):
            sent[b, place] = jnp.concatenate(
                [normed[i, :, :, : width // 2], normed[i, :, :, width // 2 :]], axis=1
            ).astype(BF16)
            for j in range(WIN):
                row = lax.rem(my_row + j, WIN)
                target = row * WIN + place
                away = pltpu.make_async_remote_copy(
                    src_ref=sent.at[b, place, row],
                    dst_ref=received.at[b, me],
                    send_sem=there_send.at[b],
                    recv_sem=there_recv.at[b],
                    device_id=device(target),
                    device_id_type=MESH,
                )
                if i or j:
                    away.start()
                else:
                    stays = pltpu.make_async_copy(
                        sent.at[b, place, row], received.at[b, me], there_recv.at[b]
                    )
                    pl.when(target == me)(stays.start)
                    pl.when(target != me)(away.start)
        for i, place in enumerate(places):
            res[b, :, place] = after[i * CELLS : (i + 1) * CELLS].reshape(WIN, WIN, width)

    def sample(b, carry):
        convolve(b)

        def part(half, carry):
            windows(b, half)
            return carry

        lax.fori_loop(0, WIN // GROUP_BATCH, part, 0)
        return carry

    pl.semaphore_wait(plane_sem, WIN - 1)
    lax.fori_loop(0, batch, sample, 0)

    out_row = iota((256, 256), 0)
    in_row = iota((256, 256), 1)
    perm[0] = jnp.where(
        in_row == (out_row & 15) * 16 + (out_row >> 7) * 8 + ((out_row >> 4) & 7), 1.0, 0.0
    ).astype(BF16)
    perm[1] = jnp.where(
        out_row == (in_row & 15) * 16 + (in_row >> 7) * 8 + ((in_row >> 4) & 7), 1.0, 0.0
    ).astype(BF16)
    fill_bias(grid_table[...], 1, spread, steps, bias)
    loads[4].wait()
    value_t[1] = dot_nt(identity(width), grid_qkv[:, 2 * width :]).astype(BF16)

    def grid(b, carry):
        pltpu.make_async_copy(received.at[b], received.at[b], there_recv.at[b]).wait()
        half_width = width // 2
        for chunk in range(4):
            rows = received[b, chunk * 16 : (chunk + 1) * 16].reshape(256, half_width)
            turned = dot_nn(perm[0], rows).astype(BF16)
            for half in range(2):
                grouped[:, chunk * 16 : (chunk + 1) * 16, half * half_width : (half + 1) * half_width] = (
                    turned[half * 128 : (half + 1) * 128].reshape(WIN, 16, half_width)
                )

        def groups(part, carry):
            start = part * 4
            x = grouped[pl.ds(start, 4)].reshape(4 * CELLS, width)
            heads = attend(x, grid_qkv, value_t, bias, 1)
            heads_buf[pl.ds(start, 4)] = heads.reshape(4, CELLS, width)
            return carry

        lax.fori_loop(0, 2, groups, 0)
        for turn in range(4):
            chunk = lax.rem(me // 16 + turn, 4)
            cut = pl.ds(pl.multiple_of(chunk * 16, 16), 16)
            rows = jnp.concatenate(
                [
                    heads_buf[:, cut, half * half_width : (half + 1) * half_width].reshape(
                        128, half_width
                    )
                    for half in range(2)
                ],
                axis=0,
            )
            answers[b, cut] = dot_nn(perm[1], rows).astype(BF16).reshape(16, 16, half_width)
            for i in range(16):
                target = chunk * 16 + lax.rem(me + i, 16)
                if turn or i:
                    pltpu.make_async_remote_copy(
                        src_ref=answers.at[b, target],
                        dst_ref=returned.at[b, me],
                        send_sem=back_send.at[b],
                        recv_sem=back_recv.at[b],
                        device_id=device(target),
                        device_id_type=MESH,
                    ).start()
                else:
                    pltpu.make_async_copy(
                        answers.at[b, me], returned.at[b, me], back_recv.at[b]
                    ).start()
        return carry

    lax.fori_loop(0, batch, grid, 0)
    loads[5].wait()
    loads[6].wait()
    loads[7].wait()
    gain = gain_ref[...]

    def mlp(step, carry):
        b = step
        pltpu.make_async_copy(returned.at[b], returned.at[b], back_recv.at[b]).wait()
        packed = returned[b].astype(F32)
        heads = jnp.concatenate([packed[:, :8], packed[:, 8:]], axis=2)
        heads = heads.reshape(8 * CELLS, width).astype(BF16)
        start = 0
        total = res[b].reshape(8 * CELLS, width) + dot_nn(heads, grid_out[...])
        normed = (layer_norm(total) * gain).astype(BF16)
        cut = 256
        for i in range(mlp_in.shape[1] // cut):
            inner = dot_nn(normed, mlp_in[:, i * cut : (i + 1) * cut])
            cubic = inner + 0.044715 * (inner * inner * inner)
            hidden = 0.5 * inner * (1.0 + jnp.tanh(math.sqrt(2.0 / math.pi) * cubic))
            total = total + dot_nn(hidden.astype(BF16), mlp_out[i * cut : (i + 1) * cut, :])
        res[b] = total.reshape(8, WIN, WIN, width)
        pltpu.make_async_copy(
            res.at[b], out_ref.at[b], out_sem
        ).start()
        return carry

    lax.fori_loop(0, batch, mlp, 0)
    for dw, dn in edges:
        pl.when(exists(dw, dn))(edge_copy(dw, dn).wait_send)
    for b in range(batch):
        for dw in (-1, 1):
            pl.when(exists(dw, 0))(row_copy(b, dw).wait_send)
    for b in range(batch):
        part = received.at[b, pl.ds(0, CELLS - 1)]
        pltpu.make_async_copy(part, part, there_send.at[b]).wait()
        pltpu.make_async_copy(part, part, back_send.at[b]).wait()
    pltpu.make_async_copy(res, out_ref, out_sem).wait()


def copy_kernel(source_ref, target_ref, held, in_sem, out_sem):
    batch, rows = held.shape[0], held.shape[1]
    pieces = [(b, pl.ds(row, 2)) for b in range(batch) for row in range(0, rows, 2)]
    loads = [
        pltpu.make_async_copy(source_ref.at[piece], held.at[piece], in_sem.at[i])
        for i, piece in enumerate(pieces)
    ]
    stores = [
        pltpu.make_async_copy(held.at[piece], target_ref.at[piece], out_sem.at[i])
        for i, piece in enumerate(pieces)
    ]
    for load in loads:
        load.start()
    for load, store in zip(loads, stores):
        load.wait()
        store.start()
    for store in stores:
        store.wait()


def on_device(
    latent,
    context,
    conv_weight,
    window_qkv,
    window_out,
    window_bias,
    grid_qkv,
    grid_out,
    grid_bias,
    mlp_gain,
    mlp_in,
    mlp_out,
):
    samples, row_count, col_count, channels = latent.shape
    tiles = latent.reshape(samples, row_count, col_count // WIN, WIN, channels)
    vmem = pltpu.VMEM
    dma = pltpu.SemaphoreType.DMA
    any_spec = pl.BlockSpec(memory_space=pl.ANY)
    vmem_spec = pl.BlockSpec(memory_space=pltpu.VMEM)
    slots = (samples, CELLS, 2 * WIN, channels // 2)
    result = pl.pallas_call(
        block_kernel,
        out_shape=jax.ShapeDtypeStruct(tiles.shape, F32),
        in_specs=[any_spec] * 9 + [vmem_spec] * 3,
        out_specs=any_spec,
        scratch_shapes=[
            vmem(tiles.shape, F32),
            vmem((samples, 8, 32, context.shape[3]), BF16),
            vmem((2, 16, context.shape[3]), BF16),
            vmem((2, 3, 16, context.shape[3]), BF16),
            vmem(conv_weight.shape, BF16),
            vmem(window_qkv.shape, BF16),
            vmem(window_out.shape, BF16),
            vmem(grid_qkv.shape, BF16),
            vmem(grid_out.shape, BF16),
            vmem(mlp_in.shape, BF16),
            vmem(mlp_out.shape, BF16),
            vmem((2, channels, channels), BF16),
            vmem((row_count * col_count, 6 * CTX_COLS), BF16),
            vmem((2, 4, CELLS, 256), F32),
            vmem((240, 1024), F32),
            vmem((15, 8, 1024), F32),
            vmem((2, 256, 256), BF16),
            vmem((samples, WIN, WIN, 2 * WIN, channels // 2), BF16),
            vmem(slots, BF16),
            vmem(slots, BF16),
            vmem(slots, BF16),
            vmem((WIN, CELLS, channels), BF16),
            vmem((WIN, CELLS, channels), BF16),
            dma((8,)),
            dma,
            dma((samples, 2)),
            dma((samples, 2)),
            dma((2, 3)),
            dma((2, 3)),
            dma((samples,)),
            dma((samples,)),
            dma((samples,)),
            dma((samples,)),
            dma,
            pltpu.SemaphoreType.REGULAR,
        ],
        compiler_params=pltpu.CompilerParams(
            collective_id=0, has_side_effects=True, vmem_limit_bytes=56 * 2**20
        ),
        cost_estimate=pl.CostEstimate(
            flops=10_000_000_000, bytes_accessed=16_000_000, transcendentals=4_000_000
        ),
    )(
        tiles,
        context,
        conv_weight,
        window_qkv,
        window_out,
        grid_qkv,
        grid_out,
        mlp_in,
        mlp_out,
        window_bias.transpose(1, 0, 2),
        grid_bias.transpose(1, 0, 2),
        mlp_gain.reshape(1, channels),
    )
    result = pl.pallas_call(
        copy_kernel,
        out_shape=jax.ShapeDtypeStruct(tiles.shape, F32),
        in_specs=[any_spec],
        out_specs=any_spec,
        scratch_shapes=[vmem(tiles.shape, F32), dma((4 * samples,)), dma((4 * samples,))],
        compiler_params=pltpu.CompilerParams(vmem_limit_bytes=56 * 2**20),
    )(result)
    return result.reshape(latent.shape)


def solution(mesh):
    return jax.shard_map(
        on_device,
        mesh=mesh,
        in_specs=(
            P(None, "wide", "narrow", None),
            P(None, "wide", "narrow", None),
            P(),
            P(),
            P(),
            P(),
            P(),
            P(),
            P(),
            P(),
            P(),
            P(),
        ),
        out_specs=P(None, "wide", "narrow", None),
        check_vma=False,
    )
```

```python
import math

import jax
import jax.numpy as jnp
from jax import lax
from jax.experimental import pallas as pl
from jax.experimental.pallas import tpu as pltpu
from jax.sharding import PartitionSpec as P

MESH = pl.DeviceIdType.MESH
F32 = jnp.float32
BF16 = jnp.bfloat16
NORM_EPS = 1e-05
HEAD = 32
WIN = 8
CELLS = WIN * WIN
LOG2E = 1.4426950408889634
CTX_COLS = 48
GROUP_BATCH = 4


def iota(shape, dim):
    return lax.broadcasted_iota(jnp.int32, shape, dim)


def dot_nn(a, b):
    return jnp.dot(a, b, preferred_element_type=F32)


def dot_nt(a, b):
    return lax.dot_general(a, b, (((1,), (1,)), ((), ())), preferred_element_type=F32)


def layer_norm(values):
    center = values - jnp.mean(values, axis=-1, keepdims=True)
    spread = jnp.mean(center * center, axis=-1, keepdims=True)
    return center * lax.rsqrt(spread + NORM_EPS)


def identity(size):
    return jnp.where(iota((size, size), 0) == iota((size, size), 1), 1.0, 0.0).astype(BF16)


def fill_upsampler(up_ref):
    rows, depth = up_ref.shape
    lane = iota((1, depth), 1)
    coarse_row = jnp.zeros((1, depth), jnp.int32)
    for step in range(1, depth // CTX_COLS):
        coarse_row = coarse_row + jnp.where(lane >= step * CTX_COLS, 1, 0)
    coarse_col = lane - coarse_row * CTX_COLS
    block = 64
    for start in range(0, rows, block):
        fine_row = start // 64
        row_centre = fine_row // 2 + 1
        row_other = fine_row // 2 + (2 if fine_row % 2 else 0)
        row_weight = jnp.where(coarse_row == row_centre, 0.75, 0.0) + jnp.where(
            coarse_row == row_other, 0.25, 0.0
        )
        fine_col = iota((block, depth), 0)
        col_centre = (fine_col >> 1) + 8
        col_other = col_centre + 2 * (fine_col & 1) - 1
        col_weight = jnp.where(coarse_col == col_centre, 0.75, 0.0) + jnp.where(
            coarse_col == col_other, 0.25, 0.0
        )
        up_ref[pl.ds(start, block), :] = (row_weight * col_weight).astype(BF16)


def three_terms(values):
    high = values.astype(BF16)
    rest = values - high.astype(F32)
    middle = rest.astype(BF16)
    return high, middle, (rest - middle.astype(F32)).astype(BF16)


def fill_bias(table, which, spread_ref, step_ref, bias_ref):
    turn = jnp.where(iota((16, 15), 0) == iota((16, 15), 1), 1.0, 0.0).astype(BF16)
    pick = jnp.where((iota((240, 1024), 0) & 15) == (iota((240, 1024), 1) >> 6), 1.0, 0.0)
    pick = pick.astype(BF16)
    step_of_lane = iota((16, 240), 1) >> 4
    total = jnp.zeros((240, 1024), F32)
    for term in three_terms(table.reshape(240, 15)):
        turned = dot_nt(turn, term)
        apart = [jnp.where(step_of_lane == a, turned, 0.0).astype(BF16) for a in range(15)]
        total = total + dot_nn(jnp.concatenate(apart, axis=0), pick)
    spread_ref[...] = total * LOG2E
    col_step = (iota((8, 1024), 1) & 7) - iota((8, 1024), 0) + 7

    def one_row_step(a, carry):
        rows = spread_ref[pl.ds(pl.multiple_of(a * 16, 16), 16), :]
        total = jnp.zeros((8, 1024), F32)
        for j in range(15):
            total = jnp.where(col_step == j, jnp.broadcast_to(rows[j : j + 1], (8, 1024)), total)
        step_ref[a] = total
        return carry

    lax.fori_loop(0, 15, one_row_step, 0)
    query_row = (iota((8, 1024), 1) >> 3) & 7

    def one_key_row(rq, carry):
        total = jnp.zeros((8, 1024), F32)
        for rp in range(8):
            total = jnp.where(query_row == rp, step_ref[rp - rq + 7], total)
        for block in range(4):
            bias_ref[which, block, pl.ds(pl.multiple_of(rq * 8, 8), 8), :] = total[
                :, block * 256 : (block + 1) * 256
            ]
        return carry

    lax.fori_loop(0, 8, one_key_row, 0)


def attend(x, qkv_ref, value_ref, bias_ref, which):
    width = x.shape[1]
    count = x.shape[0] // CELLS
    queries = dot_nn(x, qkv_ref[:, 0:width]).astype(BF16)
    keys = dot_nn(x, qkv_ref[:, width : 2 * width]).astype(BF16)
    values = dot_nt(value_ref[which], x).astype(BF16)
    head_of_lane = iota((CELLS, 128), 1) >> 5
    head_masks = [jnp.where(head_of_lane == h, 1.0, 0.0).astype(BF16) for h in range(4)]
    group_of_lane = iota((128, count * CELLS), 1) >> 6
    group_masks = [jnp.where(group_of_lane == g, 1.0, 0.0).astype(BF16) for g in range(count)]
    low = iota((HEAD, 128), 1) < 64
    outs = []
    for block in range(width // 128):
        lanes = slice(block * 128, (block + 1) * 128)
        bias = bias_ref[which, block]
        weights = []
        for g in range(count):
            rows = slice(g * CELLS, (g + 1) * CELLS)
            query = queries[rows, lanes]
            spread = jnp.concatenate([query * mask for mask in head_masks], axis=0)
            scores = dot_nt(keys[rows, lanes], spread) * (LOG2E * HEAD**-0.5) + bias
            lifted = jnp.exp2(scores - jnp.max(scores, axis=0, keepdims=True))
            inverse = 1.0 / jnp.sum(lifted, axis=0, keepdims=True)
            weights.append((lifted * inverse).astype(BF16))
        weight = jnp.concatenate(weights, axis=0)
        value = values[lanes]
        stacked = jnp.concatenate([value * mask for mask in group_masks], axis=0)
        blended = dot_nn(stacked, weight)
        for h in range(4):
            picked = []
            for pair in range(count // 2):
                parts = []
                for g in (2 * pair, 2 * pair + 1):
                    parts.append(
                        blended[
                            g * 128 + h * HEAD : g * 128 + (h + 1) * HEAD,
                            (h // 2) * 128 : (h // 2 + 1) * 128,
                        ]
                    )
                first, second = parts
                if h % 2 == 0:
                    picked.append(jnp.where(low, first, pltpu.roll(second, 64, 1)))
                else:
                    picked.append(jnp.where(low, pltpu.roll(first, 64, 1), second))
            outs.append(jnp.concatenate(picked, axis=1).astype(BF16))
    turned = jnp.concatenate(outs, axis=0)
    return dot_nt(identity(count * CELLS), turned).astype(BF16)


def block_kernel(
    latent_ref,
    context_ref,
    conv_hbm,
    window_qkv_hbm,
    window_out_hbm,
    grid_qkv_hbm,
    grid_out_hbm,
    mlp_in_hbm,
    mlp_out_hbm,
    window_table,
    grid_table,
    gain_ref,
    out_ref,
    res,
    halo,
    edge_out,
    edge_in,
    conv_w,
    window_qkv,
    window_out,
    grid_qkv,
    grid_out,
    mlp_in,
    mlp_out,
    value_t,
    up,
    bias,
    spread,
    steps,
    perm,
    sent,
    received,
    answers,
    returned,
    grouped,
    heads_buf,
    load_sem,
    own_sem,
    row_send,
    row_recv,
    edge_send,
    edge_recv,
    there_send,
    there_recv,
    back_send,
    back_recv,
    out_sem,
    plane_sem,
):
    wide = lax.axis_index("wide")
    narrow = lax.axis_index("narrow")
    wide_count = lax.axis_size("wide")
    narrow_count = lax.axis_size("narrow")
    planes = wide_count // WIN
    plane = lax.rem(wide, planes)
    my_row = wide // planes
    me = my_row * WIN + narrow

    def device(place):
        return ((place // WIN) * planes + plane, lax.rem(place, WIN))

    loads = [
        pltpu.make_async_copy(source, target, load_sem.at[i])
        for i, (source, target) in enumerate(
            (
                (conv_hbm, conv_w),
                (latent_ref, res),
                (window_qkv_hbm, window_qkv),
                (window_out_hbm, window_out),
                (grid_qkv_hbm, grid_qkv),
                (grid_out_hbm, grid_out),
                (mlp_in_hbm, mlp_in),
                (mlp_out_hbm, mlp_out),
            )
        )
    ]
    half_rows, half_cols = context_ref.shape[1], context_ref.shape[2]
    depth = context_ref.shape[3]
    batch = latent_ref.shape[0]
    own = pltpu.make_async_copy(context_ref, halo.at[:, pl.ds(2, half_rows)], own_sem)
    own.start()
    edge_in[...] = jnp.zeros_like(edge_in)

    barrier = pltpu.get_barrier_semaphore()

    row_peers = [my_row * WIN + lax.rem(narrow + i, WIN) for i in (1, WIN - 1, *range(2, WIN - 1))]
    column_peers = [lax.rem(my_row + i, WIN) * WIN + narrow for i in range(1, WIN)]

    def neighbour(dw, dn):
        return (
            lax.rem(wide + dw + wide_count, wide_count),
            lax.rem(narrow + dn + narrow_count, narrow_count),
        )

    for dw in (-1, 1):
        for dn in (0, -1, 1):
            pl.semaphore_signal(barrier, inc=1, device_id=neighbour(dw, dn), device_id_type=MESH)
    for place in row_peers + column_peers:
        pl.semaphore_signal(barrier, inc=1, device_id=device(place), device_id_type=MESH)
    for load in loads[:4]:
        load.start()

    own.wait()
    pl.semaphore_wait(barrier, 2 * (WIN - 1) + 6)

    def exists(dw, dn):
        return (
            (wide + dw >= 0)
            & (wide + dw < wide_count)
            & (narrow + dn >= 0)
            & (narrow + dn < narrow_count)
        )

    def row_copy(b, dw):
        lane = (dw + 1) // 2
        return pltpu.make_async_remote_copy(
            src_ref=halo.at[b, pl.ds(half_rows if dw > 0 else 2, 2)],
            dst_ref=halo.at[b, pl.ds(0 if dw > 0 else half_rows + 2, 2)],
            send_sem=row_send.at[b, lane],
            recv_sem=row_recv.at[b, lane],
            device_id=neighbour(dw, 0),
            device_id_type=MESH,
        )

    def edge_copy(dw, dn):
        side = (dn + 1) // 2
        return pltpu.make_async_remote_copy(
            src_ref=edge_out.at[side],
            dst_ref=edge_in.at[1 - side, 1 - dw],
            send_sem=edge_send.at[side, 1 - dw],
            recv_sem=edge_recv.at[1 - side, 1 - dw],
            device_id=neighbour(dw, dn),
            device_id_type=MESH,
        )

    edges = [(dw, dn) for dn in (-1, 1) for dw in (-1, 0, 1)]
    for dw in (-1, 1):
        pl.when(exists(dw, 0))(row_copy(0, dw).start)
    for side in range(2):
        strip = halo[:, 2 : 2 + half_rows, side * 16 : side * 16 + 16, :].reshape(
            batch * half_rows * 16, depth
        )
        row = iota((16, batch * half_rows * 16), 0)
        pick = iota((16, batch * half_rows * 16), 1) == (row >> 1) * 16 + (row & 1) + 14 * side
        edge_out[side] = dot_nn(jnp.where(pick, 1.0, 0.0).astype(BF16), strip).astype(BF16)
    for dw, dn in edges:
        pl.when(exists(dw, dn))(edge_copy(dw, dn).start)
    for b in range(1, batch):
        for dw in (-1, 1):
            pl.when(exists(dw, 0))(row_copy(b, dw).start)

    for place in column_peers:
        pl.semaphore_signal(plane_sem, inc=1, device_id=device(place), device_id_type=MESH)
    for load in loads[4:]:
        load.start()

    fill_bias(window_table[...], 0, spread, steps, bias)
    fill_upsampler(up)
    width = window_out.shape[0]
    loads[2].wait()
    value_t[0] = dot_nt(identity(width), window_qkv[:, 2 * width :]).astype(BF16)
    for dw, dn in edges:
        pl.when(exists(-dw, -dn))(edge_copy(dw, dn).wait_recv)
    loads[0].wait()
    loads[1].wait()
    loads[3].wait()
    def convolve(b):
        for dw in (-1, 1):
            lane = (dw + 1) // 2
            arrived = halo.at[b, pl.ds(0 if dw > 0 else half_rows + 2, 2)]
            pl.when(exists(-dw, 0))(
                pltpu.make_async_copy(arrived, arrived, row_recv.at[b, lane]).wait
            )
        sides = []
        place, taken = iota((64, 48), 0), iota((64, 48), 1)
        row, col = place >> 3, place & 7
        slot = jnp.where(row < 2, 0, jnp.where(row < 2 + half_rows, 1, 2))
        their_row = jnp.where(row < 2, row + half_rows - 2, row - 2)
        their_row = jnp.where(row < 2 + half_rows, their_row, row - 2 - half_rows)
        base = slot * 16 + b * (2 * half_rows) + their_row * 2
        for side in range(2):
            first = 6 if side == 0 else 0
            chosen = (taken == base + col - first) & (col >= first) & (col < first + 2)
            strip = dot_nn(
                jnp.where(chosen, 1.0, 0.0).astype(BF16), edge_in[side].reshape(48, depth)
            )
            sides.append(strip.reshape(8, 8, depth))
        widened = jnp.concatenate([sides[0], halo[b].astype(F32), sides[1]], axis=1)
        shape = (8, CTX_COLS, depth)
        row_place = wide * half_rows - 2 + iota(shape, 0)
        col_place = narrow * half_cols - 8 + iota(shape, 1)
        inside = (
            (row_place >= 0)
            & (row_place < wide_count * half_rows)
            & (col_place >= 0)
            & (col_place < narrow_count * half_cols)
        )
        widened = jnp.where(inside, widened, 0.0).astype(BF16)
        rows = 6 * CTX_COLS
        tall = jnp.concatenate([widened[i : i + 6].reshape(rows, depth) for i in range(3)], axis=1)
        left, centre, right = [
            dot_nn(tall, conv_w[:, dl].reshape(3 * depth, width)) for dl in range(3)
        ]
        total = centre + pltpu.roll(left, 1, 0) + pltpu.roll(right, rows - 1, 0)
        shape = (6, CTX_COLS, width)
        row_place = wide * half_rows - 1 + iota(shape, 0)
        col_place = narrow * half_cols - 8 + iota(shape, 1)
        inside = (
            (row_place >= 0)
            & (row_place < wide_count * half_rows)
            & (col_place >= 0)
            & (col_place < narrow_count * half_cols)
        )
        features = jnp.where(inside.reshape(rows, width), total, 0.0).astype(BF16)
        res[b] = res[b] + dot_nn(up[...], features).reshape(res.shape[1:])

    def windows(b, part):
        per_part = GROUP_BATCH
        places = []
        for i in range(per_part):
            turn = part * per_part + i
            places.append(lax.rem(narrow + lax.rem(turn, 4) * 2 + turn // 4, WIN))
        before = jnp.concatenate([res[b, :, place].reshape(CELLS, width) for place in places], axis=0)
        normed = layer_norm(before).astype(BF16)
        heads = attend(normed, window_qkv, value_t, bias, 0)
        after = before + dot_nn(heads, window_out[...])
        normed = layer_norm(after).reshape(per_part, WIN, WIN, width)

        @pl.when((b == 0) & (part == 0))
        def _():
            pl.semaphore_wait(plane_sem, WIN - 1)

        for i, place in enumerate(places):
            sent[b, place] = jnp.concatenate(
                [normed[i, :, :, : width // 2], normed[i, :, :, width // 2 :]], axis=1
            ).astype(BF16)
            for j in range(WIN):
                row = lax.rem(my_row + j, WIN)
                target = row * WIN + place
                away = pltpu.make_async_remote_copy(
                    src_ref=sent.at[b, place, row],
                    dst_ref=received.at[b, me],
                    send_sem=there_send.at[b],
                    recv_sem=there_recv.at[b],
                    device_id=device(target),
                    device_id_type=MESH,
                )
                if i or j:
                    away.start()
                else:
                    stays = pltpu.make_async_copy(
                        sent.at[b, place, row], received.at[b, me], there_recv.at[b]
                    )
                    pl.when(target == me)(stays.start)
                    pl.when(target != me)(away.start)
        for i, place in enumerate(places):
            res[b, :, place] = after[i * CELLS : (i + 1) * CELLS].reshape(WIN, WIN, width)

    def sample(b, carry):
        convolve(b)

        def part(half, carry):
            windows(b, half)
            return carry

        lax.fori_loop(0, WIN // GROUP_BATCH, part, 0)
        return carry

    lax.fori_loop(0, batch, sample, 0)

    out_row = iota((256, 256), 0)
    in_row = iota((256, 256), 1)
    perm[0] = jnp.where(
        in_row == (out_row & 15) * 16 + (out_row >> 7) * 8 + ((out_row >> 4) & 7), 1.0, 0.0
    ).astype(BF16)
    perm[1] = jnp.where(
        out_row == (in_row & 15) * 16 + (in_row >> 7) * 8 + ((in_row >> 4) & 7), 1.0, 0.0
    ).astype(BF16)
    fill_bias(grid_table[...], 1, spread, steps, bias)
    loads[4].wait()
    value_t[1] = dot_nt(identity(width), grid_qkv[:, 2 * width :]).astype(BF16)

    def grid(b, carry):
        pltpu.make_async_copy(received.at[b], received.at[b], there_recv.at[b]).wait()
        half_width = width // 2
        for chunk in range(4):
            rows = received[b, chunk * 16 : (chunk + 1) * 16].reshape(256, half_width)
            turned = dot_nn(perm[0], rows).astype(BF16)
            for half in range(2):
                grouped[:, chunk * 16 : (chunk + 1) * 16, half * half_width : (half + 1) * half_width] = (
                    turned[half * 128 : (half + 1) * 128].reshape(WIN, 16, half_width)
                )

        def groups(part, carry):
            start = part * 4
            x = grouped[pl.ds(start, 4)].reshape(4 * CELLS, width)
            heads = attend(x, grid_qkv, value_t, bias, 1)
            heads_buf[pl.ds(start, 4)] = heads.reshape(4, CELLS, width)
            return carry

        lax.fori_loop(0, 2, groups, 0)
        for turn in range(4):
            chunk = lax.rem(me // 16 + turn, 4)
            cut = pl.ds(pl.multiple_of(chunk * 16, 16), 16)
            rows = jnp.concatenate(
                [
                    heads_buf[:, cut, half * half_width : (half + 1) * half_width].reshape(
                        128, half_width
                    )
                    for half in range(2)
                ],
                axis=0,
            )
            answers[b, cut] = dot_nn(perm[1], rows).astype(BF16).reshape(16, 16, half_width)
            for i in range(16):
                target = chunk * 16 + lax.rem(me + i, 16)
                if turn or i:
                    pltpu.make_async_remote_copy(
                        src_ref=answers.at[b, target],
                        dst_ref=returned.at[b, me],
                        send_sem=back_send.at[b],
                        recv_sem=back_recv.at[b],
                        device_id=device(target),
                        device_id_type=MESH,
                    ).start()
                else:
                    pltpu.make_async_copy(
                        answers.at[b, me], returned.at[b, me], back_recv.at[b]
                    ).start()
        return carry

    lax.fori_loop(0, batch, grid, 0)
    loads[5].wait()
    loads[6].wait()
    loads[7].wait()
    gain = gain_ref[...]

    def mlp(step, carry):
        b = step
        pltpu.make_async_copy(returned.at[b], returned.at[b], back_recv.at[b]).wait()
        packed = returned[b].astype(F32)
        heads = jnp.concatenate([packed[:, :8], packed[:, 8:]], axis=2)
        heads = heads.reshape(8 * CELLS, width).astype(BF16)
        start = 0
        total = res[b].reshape(8 * CELLS, width) + dot_nn(heads, grid_out[...])
        normed = (layer_norm(total) * gain).astype(BF16)
        cut = 256
        for i in range(mlp_in.shape[1] // cut):
            inner = dot_nn(normed, mlp_in[:, i * cut : (i + 1) * cut])
            cubic = inner + 0.044715 * (inner * inner * inner)
            hidden = 0.5 * inner * (1.0 + jnp.tanh(math.sqrt(2.0 / math.pi) * cubic))
            total = total + dot_nn(hidden.astype(BF16), mlp_out[i * cut : (i + 1) * cut, :])
        res[b] = total.reshape(8, WIN, WIN, width)
        pltpu.make_async_copy(
            res.at[b], out_ref.at[b], out_sem
        ).start()
        return carry

    lax.fori_loop(0, batch, mlp, 0)
    for dw, dn in edges:
        pl.when(exists(dw, dn))(edge_copy(dw, dn).wait_send)
    for b in range(batch):
        for dw in (-1, 1):
            pl.when(exists(dw, 0))(row_copy(b, dw).wait_send)
    for b in range(batch):
        part = received.at[b, pl.ds(0, CELLS - 1)]
        pltpu.make_async_copy(part, part, there_send.at[b]).wait()
        pltpu.make_async_copy(part, part, back_send.at[b]).wait()
    pltpu.make_async_copy(res, out_ref, out_sem).wait()


def copy_kernel(source_ref, target_ref, held, in_sem, out_sem):
    batch, rows = held.shape[0], held.shape[1]
    pieces = [(b, pl.ds(row, 2)) for b in range(batch) for row in range(0, rows, 2)]
    loads = [
        pltpu.make_async_copy(source_ref.at[piece], held.at[piece], in_sem.at[i])
        for i, piece in enumerate(pieces)
    ]
    stores = [
        pltpu.make_async_copy(held.at[piece], target_ref.at[piece], out_sem.at[i])
        for i, piece in enumerate(pieces)
    ]
    for load in loads:
        load.start()
    for load, store in zip(loads, stores):
        load.wait()
        store.start()
    for store in stores:
        store.wait()


def on_device(
    latent,
    context,
    conv_weight,
    window_qkv,
    window_out,
    window_bias,
    grid_qkv,
    grid_out,
    grid_bias,
    mlp_gain,
    mlp_in,
    mlp_out,
):
    samples, row_count, col_count, channels = latent.shape
    tiles = latent.reshape(samples, row_count, col_count // WIN, WIN, channels)
    vmem = pltpu.VMEM
    dma = pltpu.SemaphoreType.DMA
    any_spec = pl.BlockSpec(memory_space=pl.ANY)
    vmem_spec = pl.BlockSpec(memory_space=pltpu.VMEM)
    slots = (samples, CELLS, 2 * WIN, channels // 2)
    result = pl.pallas_call(
        block_kernel,
        out_shape=jax.ShapeDtypeStruct(tiles.shape, F32),
        in_specs=[any_spec] * 9 + [vmem_spec] * 3,
        out_specs=any_spec,
        scratch_shapes=[
            vmem(tiles.shape, F32),
            vmem((samples, 8, 32, context.shape[3]), BF16),
            vmem((2, 16, context.shape[3]), BF16),
            vmem((2, 3, 16, context.shape[3]), BF16),
            vmem(conv_weight.shape, BF16),
            vmem(window_qkv.shape, BF16),
            vmem(window_out.shape, BF16),
            vmem(grid_qkv.shape, BF16),
            vmem(grid_out.shape, BF16),
            vmem(mlp_in.shape, BF16),
            vmem(mlp_out.shape, BF16),
            vmem((2, channels, channels), BF16),
            vmem((row_count * col_count, 6 * CTX_COLS), BF16),
            vmem((2, 4, CELLS, 256), F32),
            vmem((240, 1024), F32),
            vmem((15, 8, 1024), F32),
            vmem((2, 256, 256), BF16),
            vmem((samples, WIN, WIN, 2 * WIN, channels // 2), BF16),
            vmem(slots, BF16),
            vmem(slots, BF16),
            vmem(slots, BF16),
            vmem((WIN, CELLS, channels), BF16),
            vmem((WIN, CELLS, channels), BF16),
            dma((8,)),
            dma,
            dma((samples, 2)),
            dma((samples, 2)),
            dma((2, 3)),
            dma((2, 3)),
            dma((samples,)),
            dma((samples,)),
            dma((samples,)),
            dma((samples,)),
            dma,
            pltpu.SemaphoreType.REGULAR,
        ],
        compiler_params=pltpu.CompilerParams(
            collective_id=0, has_side_effects=True, vmem_limit_bytes=56 * 2**20
        ),
        cost_estimate=pl.CostEstimate(
            flops=10_000_000_000, bytes_accessed=16_000_000, transcendentals=4_000_000
        ),
    )(
        tiles,
        context,
        conv_weight,
        window_qkv,
        window_out,
        grid_qkv,
        grid_out,
        mlp_in,
        mlp_out,
        window_bias.transpose(1, 0, 2),
        grid_bias.transpose(1, 0, 2),
        mlp_gain.reshape(1, channels),
    )
    result = pl.pallas_call(
        copy_kernel,
        out_shape=jax.ShapeDtypeStruct(tiles.shape, F32),
        in_specs=[any_spec],
        out_specs=any_spec,
        scratch_shapes=[vmem(tiles.shape, F32), dma((4 * samples,)), dma((4 * samples,))],
        compiler_params=pltpu.CompilerParams(vmem_limit_bytes=56 * 2**20),
    )(result)
    return result.reshape(latent.shape)


def solution(mesh):
    return jax.shard_map(
        on_device,
        mesh=mesh,
        in_specs=(
            P(None, "wide", "narrow", None),
            P(None, "wide", "narrow", None),
            P(),
            P(),
            P(),
            P(),
            P(),
            P(),
            P(),
            P(),
            P(),
            P(),
        ),
        out_specs=P(None, "wide", "narrow", None),
        check_vma=False,
    )
```
